128 devices in a mesh: dp: 4 (over x), seq: 32 (over z, y, core).
Axes of the slice: x: 4, y: 4, z: 4, core: 2. Of those that a mesh axis runs over, the one named last changes fastest.
Arguments:
- log_rows: bfloat16 [32768, 1024], P(('dp', 'seq')), may hold values from -6 to 6
- send_order: int32 [128, 256], P(('dp', 'seq')), may hold values from 0 to 255, each once within a row
- place: int32 [128, 256], P(('dp', 'seq')), may hold values from 0 to 255, each once within a row
- hist_len: int32 [4, 2], P('dp'), may hold values from 256 to 4096, as said below
- w_in: bfloat16 [1024, 4096], replicated, may hold values from -0.1875 to 0.1875
- w_out: bfloat16 [1024, 1024], replicated, may hold values from -0.1875 to 0.1875
- cotangent: bfloat16 [32768, 1024], P(('dp', 'seq')), may hold values from -6 to 6
Outputs:
- mixed: bfloat16 [32768, 1024], P(('dp', 'seq'))
- log_grad: float32 [32768, 1024], P(('dp', 'seq'))
The draws below stay inside these ranges and needn't reach their ends.
Inputs may be any that keep to these rules, and one draw needn't show every extreme that they name: `send_order`: each row holds every number of 0 to 255 once. `place`: each row holds every number of 0 to 255 once. `hist_len`: at least one history has all 4096 events.
All inputs are finite; a program needn't handle non-finite values.
Results may differ from the reference program's by a relative error of at most 0.0075.
Values may be sent and summed in bfloat16 or wider, within the bound.
No kernel may reach another device: no remote copies, remote signals or barrier semaphores. Data moves between devices by JAX's collectives and lax.ppermute only.
A program may use at most 192 MiB of HBM per device.

```python
import math
import jax
import jax.numpy as jnp
from jax import lax

D = 1024
HEADS = 8
ROWS = 256
HEAD_DIM = 128
GROUP = 16
SEQ_LEN = 4096
USERS = 8
TOKENS = 32768
SEND = 2
N_DP = 4
N_SEQ = 32


def draw_hist_len(key, part):
    key = jax.random.fold_in(key, 11)
    draw_key, pick_key = jax.random.split(key)
    count = N_DP * (N_SEQ // GROUP)
    lengths = jax.random.randint(draw_key, (count,), ROWS, SEQ_LEN + 1)
    chosen = jax.random.randint(pick_key, (), 0, count)
    lengths = jnp.where(jnp.arange(count) == chosen, SEQ_LEN, lengths)
    return lengths.reshape(N_DP, N_SEQ // GROUP).astype(jnp.int32)


def levels(stream_key, shape, cuts, least, top_value):
    def one(dim, shards_of):
        heights = jax.random.uniform(jax.random.fold_in(jax.random.fold_in(stream_key, 6), dim), (shards_of,), jnp.float32, least / len(cuts), top_value / len(cuts))
        return jnp.repeat(jnp.exp(heights), shape[dim] // shards_of).reshape((-1,) + (1,) * (len(shape) - dim - 1))

    gain = one(*cuts[0])
    for cut in cuts[1:]:
        gain = gain * one(*cut)
    return gain


def gaussian(key, dims, deviation, reach, cuts=(), kind=jnp.bfloat16):
    level = levels(key, dims, cuts, -0.22, 0.18) if cuts else 1.0
    drawn = jax.random.normal(key, dims, jnp.float32) * deviation * level
    return jnp.minimum(jnp.maximum(drawn, -reach), reach).astype(kind)


def setup_inputs(seed: int = 0) -> dict:
    seeds = jax.random.split(jax.random.key(seed), 8)
    log_rows = gaussian(seeds[0], (TOKENS, D), 1.0, 6.0, ((0, 128),))
    send_order = jax.vmap(lambda own: jax.random.permutation(own, ROWS))(jax.random.split(seeds[1], (N_DP * N_SEQ))).reshape((N_DP * N_SEQ, ROWS)).astype(jnp.int32)
    place = jax.vmap(lambda own: jax.random.permutation(own, ROWS))(jax.random.split(seeds[2], (N_DP * N_SEQ))).reshape((N_DP * N_SEQ, ROWS)).astype(jnp.int32)
    hist_len = draw_hist_len(jax.random.fold_in(seeds[7], 71), 0)
    w_in = gaussian(seeds[4], (D, 4 * D), D ** -0.5, 0.1875)
    w_out = gaussian(seeds[5], (D, D), D ** -0.5, 0.1875)
    cotangent = gaussian(seeds[6], (TOKENS, D), 1.0, 6.0, ((0, 128),))
    return dict(log_rows=log_rows, send_order=send_order, place=place, hist_len=hist_len, w_in=w_in, w_out=w_out, cotangent=cotangent)


EPSILON = 1e-05

def silu_grad(inputs):
    sigmoid = jax.nn.sigmoid(inputs)
    return sigmoid * (1.0 + inputs * (1.0 - sigmoid))

def normalize(inputs):
    centred = inputs - lax.optimization_barrier(jnp.mean(inputs, axis=-1, keepdims=True))
    variance = lax.optimization_barrier(jnp.mean(centred * centred, axis=-1, keepdims=True))
    inverse = lax.rsqrt(variance + EPSILON)
    return (centred * inverse, inverse)

def norm_back(upstream, normed, inverse):
    return inverse * (upstream - lax.optimization_barrier(jnp.mean(upstream, axis=-1, keepdims=True)) - normed * lax.optimization_barrier(jnp.mean(upstream * normed, axis=-1, keepdims=True)))

def reference(log_rows, send_order, place, hist_len, w_in, w_out, cotangent):
    owners = N_DP * N_SEQ
    owner_ids = jnp.arange(owners, dtype=jnp.int32)[:, None]
    sender = place // SEND
    within = place % SEND
    picked = send_order[sender, owner_ids * SEND + within]
    source = (sender * ROWS + picked).reshape(-1).astype(jnp.int32)
    history = log_rows[source]
    score_scale = 1.0 / math.sqrt(HEAD_DIM)

    def group_pass(operands):
        hist_rows, length, upstream_rows = operands
        hist_f32 = hist_rows.astype(jnp.float32)
        hist_hat, hist_inv = normalize(hist_f32)
        normed = hist_hat.astype(jnp.bfloat16)
        preact = jnp.dot(normed, w_in, preferred_element_type=jnp.float32)
        activated = jax.nn.silu(preact).astype(jnp.bfloat16)
        gate_rows = activated[:, :D]
        value_heads = activated[:, D:2 * D].reshape(SEQ_LEN, HEADS, HEAD_DIM).astype(jnp.float32)
        query_heads = activated[:, 2 * D:3 * D].reshape(SEQ_LEN, HEADS, HEAD_DIM).astype(jnp.float32)
        key_heads = activated[:, 3 * D:].reshape(SEQ_LEN, HEADS, HEAD_DIM).astype(jnp.float32)
        scores = jnp.einsum('qhd,khd->hqk', query_heads, key_heads) * score_scale
        position = jnp.arange(SEQ_LEN, dtype=jnp.int32)
        allowed = ((position[None, :] <= position[:, None]) & (position[None, :] < length))[None]
        weights = jnp.where(allowed, jax.nn.silu(scores), 0.0).astype(jnp.bfloat16)
        attended = jnp.einsum('hqk,khd->qhd', weights.astype(jnp.float32), value_heads).reshape(SEQ_LEN, D)
        att_hat, att_inv = normalize(attended)
        gate_f32 = gate_rows.astype(jnp.float32)
        gated = (att_hat * gate_f32).astype(jnp.bfloat16)
        mixed_rows = (hist_f32 + jnp.dot(gated, w_out, preferred_element_type=jnp.float32)).astype(jnp.bfloat16)
        upstream = jnp.dot(upstream_rows, w_out.T, preferred_element_type=jnp.float32)
        grad_gate = upstream * att_hat
        grad_attended = norm_back(upstream * gate_f32, att_hat, att_inv).astype(jnp.bfloat16)
        grad_heads = grad_attended.reshape(SEQ_LEN, HEADS, HEAD_DIM).astype(jnp.float32)
        grad_weights = jnp.einsum('qhd,khd->hqk', grad_heads, value_heads)
        grad_scores = jnp.where(allowed, grad_weights * silu_grad(scores), 0.0).astype(jnp.bfloat16)
        grad_scores32 = grad_scores.astype(jnp.float32)
        grad_query = jnp.einsum('hqk,khd->qhd', grad_scores32, key_heads) * score_scale
        grad_key = jnp.einsum('hqk,qhd->khd', grad_scores32, query_heads) * score_scale
        grad_value = jnp.einsum('hqk,qhd->khd', weights.astype(jnp.float32), grad_heads)
        grad_act = jnp.concatenate([grad_gate, grad_value.reshape(SEQ_LEN, D), grad_query.reshape(SEQ_LEN, D), grad_key.reshape(SEQ_LEN, D)], axis=1)
        grad_pre = (grad_act * silu_grad(preact)).astype(jnp.bfloat16)
        grad_norm = jnp.dot(grad_pre, w_in.T, preferred_element_type=jnp.float32)
        grad_history = norm_back(grad_norm, hist_hat, hist_inv) + upstream_rows.astype(jnp.float32)
        return (mixed_rows, grad_history)
    mixed_groups, grad_groups = lax.map(group_pass, (history.reshape(USERS, SEQ_LEN, D), hist_len.reshape(-1), cotangent.reshape(USERS, SEQ_LEN, D)))
    mixed = mixed_groups.reshape(TOKENS, D)
    log_grad = jnp.zeros((TOKENS, D), jnp.float32).at[source].set(grad_groups.reshape(TOKENS, D))
    return (mixed, log_grad)
```

```python
import functools
import math

import jax
import jax.numpy as jnp
from jax import lax
from jax.experimental import pallas as pl
from jax.experimental.pallas import tpu as pltpu
from jax.sharding import PartitionSpec as P

HEADS = 8
GROUP = 16
EPSILON = 1e-05
HALF = 128
HEAD_DIM = 128
TILE = 2
BF16 = jnp.bfloat16
F32 = jnp.float32
VMEM = pltpu.VMEM
SMEM = pltpu.SMEM


def params(limit=48 * 1024 * 1024, **kw):
    return pltpu.CompilerParams(vmem_limit_bytes=limit, **kw)


def vspec():
    return pl.BlockSpec(memory_space=VMEM)


def sspec():
    return pl.BlockSpec(memory_space=SMEM)


def dot(a, b):
    return jnp.dot(a, b, preferred_element_type=F32)


def dot_nt(a, b):
    return lax.dot_general(a, b, (((1,), (1,)), ((), ())), preferred_element_type=F32)


def dot_tn(a, b):
    return lax.dot_general(a, b, (((0,), (0,)), ((), ())), preferred_element_type=F32)


def onehot(order):
    count = order.shape[1]
    spots = lax.broadcasted_iota(jnp.int32, (count, count), 0)
    return jnp.where(spots == order, 1.0, 0.0).astype(BF16)


def row_mean(x):
    return jnp.mean(x, axis=-1, keepdims=True)


def normalize(inputs):
    centred = inputs - row_mean(inputs)
    inverse = lax.rsqrt(row_mean(centred * centred) + EPSILON)
    return centred * inverse, inverse


def pick_kernel(rows_ref, order_ref, out_ref):
    out_ref[...] = dot_tn(onehot(order_ref[...]), rows_ref[...]).astype(out_ref.dtype)


def pick_rows(rows, order):
    return pl.pallas_call(
        pick_kernel,
        out_shape=jax.ShapeDtypeStruct(rows.shape, rows.dtype),
        in_specs=[vspec(), vspec()],
        out_specs=vspec(),
        compiler_params=params(),
        name="pick_rows",
    )(rows, order)


def unpick_kernel(rows_ref, order_ref, out_ref):
    out_ref[...] = dot(onehot(order_ref[...]), rows_ref[...]).astype(out_ref.dtype)


def unpick_rows(rows, order, dtype):
    return pl.pallas_call(
        unpick_kernel,
        out_shape=jax.ShapeDtypeStruct(rows.shape, dtype),
        in_specs=[vspec(), vspec()],
        out_specs=vspec(),
        compiler_params=params(),
        name="unpick_rows",
    )(rows, order)


def project_kernel(
    info, arrived_ref, place_ref, w_ref, up_ref, hist_ref, gate_ref, slope_ref, buf_ref, normed_ref
):
    step = pl.program_id(0)
    odd = info[1] % 2

    @pl.when(step == 0)
    def _():
        history = dot_tn(onehot(place_ref[...]), arrived_ref[...])
        hist_ref[...] = history.astype(BF16)
        normed_ref[...] = normalize(history)[0].astype(BF16)

    preact = dot(normed_ref[...], w_ref[...])
    sigmoid = jax.nn.sigmoid(preact)
    act = preact * sigmoid
    slope_ref[...] = (sigmoid * (1.0 + preact * (1.0 - sigmoid))).astype(BF16)
    act = act.astype(BF16)

    def lay(part, block):
        for half in range(2):
            for head in range(HEADS):
                buf_ref[2 * head + (half ^ odd), part] = block[
                    half * HALF : (half + 1) * HALF, head * HEAD_DIM : (head + 1) * HEAD_DIM
                ]

    @pl.when(step == 0)
    def _():
        gate_ref[...] = act
        lay(3, (up_ref[...] * act.astype(F32)).astype(BF16))

    @pl.when(step == 1)
    def _():
        lay(1, act)

    @pl.when(step == 2)
    def _():
        lay(2, act)

    @pl.when(step == 3)
    def _():
        lay(0, act)


def project(info, arrived, place, w_in, upstream):
    rows, width = arrived.shape

    def whole(*shape):
        return pl.BlockSpec(shape, lambda j, *_: (0,) * len(shape))

    return pl.pallas_call(
        project_kernel,
        grid_spec=pltpu.PrefetchScalarGridSpec(
            num_scalar_prefetch=1,
            grid=(4,),
            in_specs=[
                whole(rows, width),
                whole(1, rows),
                pl.BlockSpec((width, width), lambda j, *_: (0, j)),
                whole(rows, width),
            ],
            out_specs=[
                whole(rows, width),
                whole(rows, width),
                pl.BlockSpec((rows, width), lambda j, *_: (0, j)),
                whole(GROUP, 4, HALF, HEAD_DIM),
            ],
            scratch_shapes=[VMEM((rows, width), BF16)],
        ),
        out_shape=[
            jax.ShapeDtypeStruct((rows, width), BF16),
            jax.ShapeDtypeStruct((rows, width), BF16),
            jax.ShapeDtypeStruct((rows, 4 * width), BF16),
            jax.ShapeDtypeStruct((GROUP, 4, HALF, HEAD_DIM), BF16),
        ],
        compiler_params=params(),
        name="project",
    )(info, arrived, place, w_in, upstream)


def lay_keys(info, mine_ref, other_ref, part, out_ref):
    length, core = info[0], info[2]
    spots = lax.broadcasted_iota(jnp.int32, (HALF, HEAD_DIM), 0)
    for owner in range(GROUP):
        for source, half in ((mine_ref, core ^ (owner & 1)), (other_ref, 1 - (core ^ (owner & 1)))):
            start = pl.multiple_of(owner * 2 * HALF + half * HALF, HALF)
            rows = source[owner, part].astype(F32)
            rows = jnp.where(spots + start < length, rows, 0.0)
            out_ref[pl.ds(start, HALF), :] = rows.astype(BF16)


def half_position(core, index):
    chunk = index >> 7
    return chunk * 2 * HALF + (core ^ (chunk & 1)) * HALF + (index & (HALF - 1))


def forward_kernel(info, mine_ref, other_ref, att_ref, stats_ref, key_ref, value_ref, sum_ref):
    query_tile, key_tile = TILE * HALF, TILE * 2 * HALF
    tiles = GROUP // TILE
    length, core = info[0], info[2]
    lay_keys(info, mine_ref, other_ref, 0, key_ref)
    lay_keys(info, mine_ref, other_ref, 1, value_ref)
    scale = 0.5 / math.sqrt(HEAD_DIM)
    live = (length + key_tile - 1) // key_tile

    def term(queries, j, masked):
        keys = pl.ds(pl.multiple_of(j * key_tile, key_tile), key_tile)
        half_scores = dot_nt(queries, key_ref[keys, :]) * scale
        weights = half_scores * jnp.tanh(half_scores) + half_scores
        if masked:
            query_spot = half_position(
                core, lax.broadcasted_iota(jnp.int32, (query_tile, key_tile), 0)
            )
            key_spot = lax.broadcasted_iota(jnp.int32, (query_tile, key_tile), 1)
            weights = jnp.where(key_spot <= query_spot, weights, 0.0)
        return dot(weights.astype(BF16), value_ref[keys, :])

    def query_turn(i, carry):
        queries = mine_ref[pl.ds(i * TILE, TILE), 2].reshape(query_tile, HEAD_DIM)
        sum_ref[...] = jnp.zeros_like(sum_ref)

        def key_turn(j, carry):
            sum_ref[...] += term(queries, j, False)
            return carry

        lax.fori_loop(0, jnp.minimum(i, live), key_turn, 0)

        @pl.when(i < live)
        def _():
            sum_ref[...] += term(queries, i, True)

        att = sum_ref[...].T
        up = (
            mine_ref[pl.ds(i * TILE, TILE), 3].reshape(query_tile, HEAD_DIM).astype(F32).T
        )
        where = pl.ds(pl.multiple_of(i * query_tile, query_tile), query_tile)
        att_ref[:, where] = att
        mean = jnp.mean(att, axis=0, keepdims=True)
        centred = att - mean
        stats = jnp.concatenate(
            [
                mean,
                jnp.sum(centred * centred, axis=0, keepdims=True),
                jnp.sum(up, axis=0, keepdims=True),
                jnp.sum(up * centred, axis=0, keepdims=True),
            ],
            axis=0,
        )
        for head in range(HEADS):
            stats_ref[head, :, where] = stats
        return carry

    lax.fori_loop(0, tiles, query_turn, 0)


def forward(info, mine, other):
    half = GROUP * HALF
    return pl.pallas_call(
        forward_kernel,
        out_shape=[
            jax.ShapeDtypeStruct((HEAD_DIM, half), F32),
            jax.ShapeDtypeStruct((HEADS, 4, half), F32),
        ],
        in_specs=[sspec(), vspec(), vspec()],
        out_specs=[vspec(), vspec()],
        scratch_shapes=[
            VMEM((2 * half, HEAD_DIM), BF16),
            VMEM((2 * half, HEAD_DIM), BF16),
            VMEM((TILE * HALF, HEAD_DIM), F32),
        ],
        compiler_params=params(),
        name="forward",
    )(info, mine, other)


def backward_kernel(
    info,
    mine_ref,
    other_ref,
    att_ref,
    stats_ref,
    out_ref,
    own_ref,
    sib_ref,
    key_ref,
    key_t_ref,
    value_ref,
    query_t_ref,
    grad_ref,
    grad_t_ref,
    dq_ref,
    dk_ref,
    dv_ref,
):
    query_tile, key_tile = TILE * HALF, TILE * 2 * HALF
    tiles = GROUP // TILE
    length, core = info[0], info[2]
    width = HEADS * HEAD_DIM
    lay_keys(info, mine_ref, other_ref, 0, key_ref)
    lay_keys(info, mine_ref, other_ref, 1, value_ref)
    scale = 0.5 / math.sqrt(HEAD_DIM)
    live = (length + key_tile - 1) // key_tile

    stat = [[stats_ref[head, s : s + 1, :] for s in range(4)] for head in range(HEADS)]
    mean = sum(row[0] for row in stat) * (1.0 / HEADS)
    square = sum(row[1] + HEAD_DIM * (row[0] - mean) * (row[0] - mean) for row in stat)
    inverse = lax.rsqrt(square * (1.0 / width) + EPSILON)
    up_mean = sum(row[2] for row in stat) * (1.0 / width)
    cross = sum(row[3] + (row[0] - mean) * row[2] for row in stat) * inverse * (1.0 / width)

    for chunk in range(GROUP):
        where = slice(chunk * HALF, (chunk + 1) * HALF)
        up = mine_ref[chunk, 3].astype(F32).T
        hat = (att_ref[:, where] - mean[:, where]) * inverse[:, where]
        out_ref[chunk, 3] = hat.T.astype(BF16)
        grad = inverse[:, where] * (up - up_mean[:, where] - hat * cross[:, where])
        grad_t_ref[:, where] = grad.astype(BF16)
        grad_ref[where, :] = grad.T.astype(BF16)
        query_t_ref[:, where] = mine_ref[chunk, 2].astype(F32).T.astype(BF16)
    for block in range(2 * GROUP):
        where = slice(block * HALF, (block + 1) * HALF)
        key_t_ref[:, where] = key_ref[where, :].astype(F32).T.astype(BF16)

    dq_ref[...] = jnp.zeros_like(dq_ref)
    dk_ref[...] = jnp.zeros_like(dk_ref)
    dv_ref[...] = jnp.zeros_like(dv_ref)

    def term(i, j, masked):
        keys = pl.ds(pl.multiple_of(j * key_tile, key_tile), key_tile)
        rows = pl.ds(pl.multiple_of(i * query_tile, query_tile), query_tile)
        half_scores = dot(key_ref[keys, :], query_t_ref[:, rows]) * scale
        grad_weights = dot(value_ref[keys, :], grad_t_ref[:, rows])
        plus = jnp.tanh(half_scores) + 1.0
        weights = half_scores * plus
        slope = plus * ((half_scores + half_scores + 1.0) - weights)
        grad_scores = grad_weights * slope
        if masked:
            query_spot = half_position(
                core, lax.broadcasted_iota(jnp.int32, (key_tile, query_tile), 1)
            )
            key_spot = lax.broadcasted_iota(jnp.int32, (key_tile, query_tile), 0)
            allowed = key_spot <= query_spot
            weights = jnp.where(allowed, weights, 0.0)
            grad_scores = jnp.where(allowed, grad_scores, 0.0)
        weights = weights.astype(BF16)
        grad_scores = grad_scores.astype(BF16)
        dv_ref[keys, :] += dot(weights, grad_ref[rows, :])
        queries = mine_ref[pl.ds(i * TILE, TILE), 2].reshape(query_tile, HEAD_DIM)
        dk_ref[keys, :] += dot(grad_scores, queries)
        dq_ref[:, rows] += dot(key_t_ref[:, keys], grad_scores)

    def key_turn(j, carry):
        def query_turn(i, carry):
            term(i, j, False)
            return carry

        term(j, j, True)
        lax.fori_loop(j + 1, tiles, query_turn, 0)
        return carry

    lax.fori_loop(0, live, key_turn, 0)

    for owner in range(GROUP):
        where = slice(owner * HALF, (owner + 1) * HALF)
        out_ref[owner, 2] = (dq_ref[:, where].T * scale).astype(BF16)
        half = core ^ (owner & 1)
        kept = pl.ds(pl.multiple_of(owner * 2 * HALF + half * HALF, HALF), HALF)
        sent = pl.ds(pl.multiple_of(owner * 2 * HALF + (1 - half) * HALF, HALF), HALF)
        own_ref[owner, 0] = dk_ref[kept, :] * scale
        own_ref[owner, 1] = dv_ref[kept, :]
        sib_ref[owner, 0] = (dk_ref[sent, :] * scale).astype(BF16)
        sib_ref[owner, 1] = dv_ref[sent, :].astype(BF16)


def backward(info, mine, other, att, stats):
    half = GROUP * HALF
    return pl.pallas_call(
        backward_kernel,
        out_shape=[
            jax.ShapeDtypeStruct((GROUP, 4, HALF, HEAD_DIM), BF16),
            jax.ShapeDtypeStruct((GROUP, 2, HALF, HEAD_DIM), F32),
            jax.ShapeDtypeStruct((GROUP, 2, HALF, HEAD_DIM), BF16),
        ],
        in_specs=[sspec(), vspec(), vspec(), vspec(), vspec()],
        out_specs=[vspec(), vspec(), vspec()],
        scratch_shapes=[
            VMEM((2 * half, HEAD_DIM), BF16),
            VMEM((HEAD_DIM, 2 * half), BF16),
            VMEM((2 * half, HEAD_DIM), BF16),
            VMEM((HEAD_DIM, half), BF16),
            VMEM((half, HEAD_DIM), BF16),
            VMEM((HEAD_DIM, half), BF16),
            VMEM((HEAD_DIM, half), F32),
            VMEM((2 * half, HEAD_DIM), F32),
            VMEM((2 * half, HEAD_DIM), F32),
        ],
        compiler_params=params(),
        name="backward",
    )(info, mine, other, att, stats)


def merge_kernel(out_ref, own_ref, sib_ref, done_ref):
    done_ref[:, 0:2] = (own_ref[...] + sib_ref[...].astype(F32)).astype(BF16)
    done_ref[:, 2:4] = out_ref[:, 2:4]


def merge(out, own, sib):
    block = 4
    return pl.pallas_call(
        merge_kernel,
        grid=(GROUP // block,),
        in_specs=[
            pl.BlockSpec((block, 4, HALF, HEAD_DIM), lambda i: (i, 0, 0, 0)),
            pl.BlockSpec((block, 2, HALF, HEAD_DIM), lambda i: (i, 0, 0, 0)),
            pl.BlockSpec((block, 2, HALF, HEAD_DIM), lambda i: (i, 0, 0, 0)),
        ],
        out_specs=pl.BlockSpec((block, 4, HALF, HEAD_DIM), lambda i: (i, 0, 0, 0)),
        out_shape=jax.ShapeDtypeStruct(out.shape, out.dtype),
        compiler_params=params(),
        name="merge",
    )(out, own, sib)


def finish_kernel(
    info,
    back_ref,
    gate_ref,
    slope_ref,
    hist_ref,
    up_ref,
    cot_ref,
    place_ref,
    w_in_ref,
    w_out_ref,
    mixed_ref,
    rows_ref,
    part_ref,
    total_ref,
):
    step = pl.program_id(0)
    odd = info[1] % 2

    def gather(part):
        for half in range(2):
            for head in range(HEADS):
                part_ref[
                    half * HALF : (half + 1) * HALF, head * HEAD_DIM : (head + 1) * HEAD_DIM
                ] = back_ref[2 * head + (half ^ odd), part]
        return part_ref[...].astype(F32)

    def add(grad):
        pre = (grad * slope_ref[...].astype(F32)).astype(BF16)
        return dot_nt(pre, w_in_ref[...])

    @pl.when(step == 0)
    def _():
        hat = gather(3)
        gated = (hat * gate_ref[...].astype(F32)).astype(BF16)
        mixed_ref[...] = (hist_ref[...].astype(F32) + dot(gated, w_out_ref[...])).astype(BF16)
        total_ref[...] = add(up_ref[...] * hat)

    for s, part in ((1, 1), (2, 2), (3, 0)):

        @pl.when(step == s)
        def _():
            total_ref[...] += add(gather(part))

    @pl.when(step == 3)
    def _():
        hat, inverse = normalize(hist_ref[...].astype(F32))
        grad = total_ref[...]
        grad = inverse * (grad - row_mean(grad) - hat * row_mean(grad * hat))
        grad = (grad + cot_ref[...].astype(F32)).astype(BF16)
        rows_ref[...] = dot(onehot(place_ref[...]), grad).astype(BF16)


def finish(info, back, gate, slope, history, upstream, cotangent, place, w_in, w_out):
    rows, width = history.shape

    def whole(*shape):
        return pl.BlockSpec(shape, lambda j, *_: (0,) * len(shape))

    return pl.pallas_call(
        finish_kernel,
        grid_spec=pltpu.PrefetchScalarGridSpec(
            num_scalar_prefetch=1,
            grid=(4,),
            in_specs=[
                whole(GROUP, 4, HALF, HEAD_DIM),
                whole(rows, width),
                pl.BlockSpec((rows, width), lambda j, *_: (0, j)),
                whole(rows, width),
                whole(rows, width),
                whole(rows, width),
                whole(1, rows),
                pl.BlockSpec((width, width), lambda j, *_: (0, j)),
                whole(width, width),
            ],
            out_specs=[whole(rows, width), whole(rows, width)],
            scratch_shapes=[VMEM((rows, width), BF16), VMEM((rows, width), F32)],
        ),
        out_shape=[
            jax.ShapeDtypeStruct((rows, width), BF16),
            jax.ShapeDtypeStruct((rows, width), BF16),
        ],
        compiler_params=params(),
        name="finish",
    )(info, back, gate, slope, history, upstream, cotangent, place, w_in, w_out)


def body(log_rows, send_order, place, hist_len, w_in, w_out, cotangent):
    rows, width = log_rows.shape
    seq_size = lax.axis_size("seq")
    seq_index = lax.axis_index("seq")
    spot = seq_index % GROUP
    length = jnp.take(hist_len[0], seq_index // GROUP)
    info = jnp.stack([length, spot, spot % 2]).astype(jnp.int32)
    groups = [list(range(g, g + GROUP)) for g in range(0, seq_size, GROUP)]
    same_core = [list(range(g + c, g + GROUP, 2)) for g in range(0, seq_size, GROUP) for c in (0, 1)]
    swap = [(i, i ^ 1) for i in range(seq_size)]

    def to_all(block):
        block = block.reshape(rows // 2, 2, width)
        block = lax.all_to_all(block, ("dp", "seq"), split_axis=0, concat_axis=0, tiled=True)
        return block.reshape(rows, width)

    def to_group(block, members):
        return lax.all_to_all(
            block, "seq", split_axis=0, concat_axis=0, tiled=True, axis_index_groups=members
        )

    upstream = jnp.dot(cotangent, w_out.T, preferred_element_type=F32)
    arrived = to_all(pick_rows(log_rows, send_order))
    history, gate, slope, block = project(info, arrived, place, w_in, upstream)
    mine = to_group(block, groups)
    other = lax.ppermute(mine[:, :2], "seq", swap)
    att, stats = forward(info, mine, other)
    stats = to_group(stats, same_core)
    out, own, sib = backward(info, mine, other, att, stats)
    sib = lax.ppermute(sib, "seq", swap)
    back = to_group(merge(out, own, sib), groups)
    mixed, grads = finish(
        info, back, gate, slope, history, upstream, cotangent, place, w_in, w_out
    )
    log_grad = unpick_rows(to_all(grads), send_order, F32)
    return (mixed, log_grad)


def solution(mesh):
    rows = P(("dp", "seq"), None)
    return jax.shard_map(
        body,
        mesh=mesh,
        in_specs=(rows, rows, rows, P("dp", None), P(), P(), rows),
        out_specs=(rows, rows),
        check_vma=False,
    )
```

```python
import functools
import math

import jax
import jax.numpy as jnp
from jax import lax
from jax.experimental import pallas as pl
from jax.experimental.pallas import tpu as pltpu
from jax.sharding import PartitionSpec as P

HEADS = 8
GROUP = 16
EPSILON = 1e-05
CHIPS = 8
ROWS = 256
HEAD_DIM = 128
BF16 = jnp.bfloat16
F32 = jnp.float32
VMEM = pltpu.VMEM
SMEM = pltpu.SMEM


def params(limit=48 * 1024 * 1024, **kw):
    return pltpu.CompilerParams(vmem_limit_bytes=limit, **kw)


def vspec():
    return pl.BlockSpec(memory_space=VMEM)


def sspec():
    return pl.BlockSpec(memory_space=SMEM)


def dot(a, b):
    return jnp.dot(a, b, preferred_element_type=F32)


def dot_nt(a, b):
    return lax.dot_general(a, b, (((1,), (1,)), ((), ())), preferred_element_type=F32)


def dot_tn(a, b):
    return lax.dot_general(a, b, (((0,), (0,)), ((), ())), preferred_element_type=F32)


def onehot(order):
    count = order.shape[1]
    spots = lax.broadcasted_iota(jnp.int32, (count, count), 0)
    return jnp.where(spots == order, 1.0, 0.0).astype(BF16)


def row_mean(x):
    return jnp.mean(x, axis=-1, keepdims=True)


def normalize(inputs):
    centred = inputs - row_mean(inputs)
    inverse = lax.rsqrt(row_mean(centred * centred) + EPSILON)
    return centred * inverse, inverse


def pick_kernel(rows_ref, order_ref, out_ref):
    out_ref[...] = dot_tn(onehot(order_ref[...]), rows_ref[...]).astype(out_ref.dtype)


def pick_rows(rows, order):
    return pl.pallas_call(
        pick_kernel,
        out_shape=jax.ShapeDtypeStruct(rows.shape, rows.dtype),
        in_specs=[vspec(), vspec()],
        out_specs=vspec(),
        compiler_params=params(),
        name="pick_rows",
    )(rows, order)


def unpick_kernel(rows_ref, order_ref, out_ref):
    out_ref[...] = dot(onehot(order_ref[...]), rows_ref[...]).astype(out_ref.dtype)


def unpick_rows(rows, order, dtype):
    return pl.pallas_call(
        unpick_kernel,
        out_shape=jax.ShapeDtypeStruct(rows.shape, dtype),
        in_specs=[vspec(), vspec()],
        out_specs=vspec(),
        compiler_params=params(),
        name="unpick_rows",
    )(rows, order)


def project_kernel(
    arrived_ref, place_ref, w_ref, up_ref, hist_ref, gate_ref, slope_ref, buf_ref, normed_ref
):
    step = pl.program_id(0)

    @pl.when(step == 0)
    def _():
        history = dot_tn(onehot(place_ref[...]), arrived_ref[...])
        hist_ref[...] = history.astype(BF16)
        normed_ref[...] = normalize(history)[0].astype(BF16)

    preact = dot(normed_ref[...], w_ref[...])
    sigmoid = jnp.tanh(preact * 0.5) * 0.5 + 0.5
    act = preact * sigmoid
    slope_ref[...] = (sigmoid + act - act * sigmoid).astype(BF16)
    act = act.astype(BF16)

    def lay(part, block):
        for head in range(HEADS):
            buf_ref[head, part] = block[:, head * HEAD_DIM : (head + 1) * HEAD_DIM]

    @pl.when(step == 0)
    def _():
        gate_ref[...] = act
        lay(3, (up_ref[...] * act.astype(F32)).astype(BF16))

    @pl.when(step == 1)
    def _():
        lay(1, act)

    @pl.when(step == 2)
    def _():
        lay(2, act)

    @pl.when(step == 3)
    def _():
        lay(0, act)


def project(arrived, place, w_in, upstream):
    rows, width = arrived.shape

    def whole(*shape):
        return pl.BlockSpec(shape, lambda j, *_: (0,) * len(shape))

    return pl.pallas_call(
        project_kernel,
        grid_spec=pltpu.PrefetchScalarGridSpec(
            num_scalar_prefetch=0,
            grid=(4,),
            in_specs=[
                whole(rows, width),
                whole(1, rows),
                pl.BlockSpec((width, width), lambda j, *_: (0, j)),
                whole(rows, width),
            ],
            out_specs=[
                whole(rows, width),
                whole(rows, width),
                pl.BlockSpec((rows, width), lambda j, *_: (0, j)),
                whole(CHIPS, 4, ROWS, HEAD_DIM),
            ],
            scratch_shapes=[VMEM((rows, width), BF16)],
        ),
        out_shape=[
            jax.ShapeDtypeStruct((rows, width), BF16),
            jax.ShapeDtypeStruct((rows, width), BF16),
            jax.ShapeDtypeStruct((rows, 4 * width), BF16),
            jax.ShapeDtypeStruct((CHIPS, 4, ROWS, HEAD_DIM), BF16),
        ],
        compiler_params=params(),
        name="project",
    )(arrived, place, w_in, upstream)


def lay_keys(info, mine_ref, other_ref, part, out_ref):
    length, core = info[0], info[2]
    for chip in range(CHIPS):
        for source, side in ((mine_ref, core), (other_ref, 1 - core)):
            start = pl.multiple_of((2 * chip + side) * ROWS, ROWS)
            out_ref[pl.ds(start, ROWS), :] = source[chip, part]

    @pl.when(length < GROUP * ROWS)
    def _():
        def clear(block, carry):
            where = pl.ds(pl.multiple_of(block * ROWS, ROWS), ROWS)
            spots = lax.broadcasted_iota(jnp.int32, (ROWS, HEAD_DIM), 0) + block * ROWS
            rows = jnp.where(spots < length, out_ref[where, :].astype(F32), 0.0)
            out_ref[where, :] = rows.astype(BF16)
            return carry

        lax.fori_loop(length // ROWS, GROUP, clear, 0)


def forward_kernel(info, mine_ref, other_ref, att_ref, stats_ref, key_ref, value_ref, sum_ref):
    many, key_tile = 4, 1024
    query_tile = many * ROWS
    length, core = info[0], info[2]
    lay_keys(info, mine_ref, other_ref, 0, key_ref)
    lay_keys(info, mine_ref, other_ref, 1, value_ref)
    scale = 0.5 / math.sqrt(HEAD_DIM)

    def weigh(queries, keys):
        half_scores = dot_nt(queries, keys) * scale
        return half_scores * jnp.tanh(half_scores) + half_scores

    def whole(queries, start, size):
        keys = pl.ds(pl.multiple_of(start, ROWS), size)
        return dot(weigh(queries, key_ref[keys, :]).astype(BF16), value_ref[keys, :])

    def query_turn(n, carry):
        queries = mine_ref[pl.ds(n * many, many), 2].reshape(query_tile, HEAD_DIM)
        sum_ref[...] = jnp.zeros_like(sum_ref)
        base = n * many * 2 * ROWS

        def key_turn(j, carry):
            sum_ref[...] += whole(queries, j * key_tile, key_tile)
            return carry

        live = (length + key_tile - 1) // key_tile
        lax.fori_loop(0, jnp.minimum(base // key_tile, live), key_turn, 0)

        @pl.when(base < length)
        def _():
            for g in range(many):
                rows = slice(g * ROWS, (g + 1) * ROWS)
                block = mine_ref[n * many + g, 2]
                if g:
                    sum_ref[rows, :] += whole(block, base, 2 * ROWS * g)
                keys = pl.ds(pl.multiple_of(base + 2 * ROWS * g, ROWS), 2 * ROWS)
                query_spot = lax.broadcasted_iota(jnp.int32, (ROWS, 2 * ROWS), 0) + core * ROWS
                key_spot = lax.broadcasted_iota(jnp.int32, (ROWS, 2 * ROWS), 1)
                weights = jnp.where(key_spot <= query_spot, weigh(block, key_ref[keys, :]), 0.0)
                sum_ref[rows, :] += dot(weights.astype(BF16), value_ref[keys, :])

        att = sum_ref[...].T
        up = mine_ref[pl.ds(n * many, many), 3].reshape(query_tile, HEAD_DIM).astype(F32).T
        where = pl.ds(pl.multiple_of(n * query_tile, query_tile), query_tile)
        att_ref[:, where] = att
        mean = jnp.mean(att, axis=0, keepdims=True)
        centred = att - mean
        stats = jnp.concatenate(
            [
                mean,
                jnp.sum(centred * centred, axis=0, keepdims=True),
                jnp.sum(up, axis=0, keepdims=True),
                jnp.sum(up * centred, axis=0, keepdims=True),
            ],
            axis=0,
        )
        for head in range(HEADS):
            stats_ref[head, :, where] = stats
        return carry

    lax.fori_loop(0, CHIPS // many, query_turn, 0)


def forward(info, mine, other):
    half = CHIPS * ROWS
    return pl.pallas_call(
        forward_kernel,
        out_shape=[
            jax.ShapeDtypeStruct((HEAD_DIM, half), F32),
            jax.ShapeDtypeStruct((HEADS, 4, half), F32),
        ],
        in_specs=[sspec(), vspec(), vspec()],
        out_specs=[vspec(), vspec()],
        scratch_shapes=[
            VMEM((2 * half, HEAD_DIM), BF16),
            VMEM((2 * half, HEAD_DIM), BF16),
            VMEM((4 * ROWS, HEAD_DIM), F32),
        ],
        compiler_params=params(),
        name="forward",
    )(info, mine, other)


def backward_kernel(
    info,
    mine_ref,
    other_ref,
    att_ref,
    stats_ref,
    out_ref,
    sib_ref,
    key_ref,
    key_t_ref,
    value_ref,
    query_t_ref,
    grad_ref,
    grad_t_ref,
    dq_ref,
    dk_ref,
    dv_ref,
):
    key_tile = 2 * ROWS
    length, core = info[0], info[2]
    width = HEADS * HEAD_DIM
    lay_keys(info, mine_ref, other_ref, 0, key_ref)
    lay_keys(info, mine_ref, other_ref, 1, value_ref)
    scale = 0.5 / math.sqrt(HEAD_DIM)

    stat = [[stats_ref[head, s : s + 1, :] for s in range(4)] for head in range(HEADS)]
    mean = sum(row[0] for row in stat) * (1.0 / HEADS)
    square = sum(row[1] + HEAD_DIM * (row[0] - mean) * (row[0] - mean) for row in stat)
    inverse = lax.rsqrt(square * (1.0 / width) + EPSILON)
    up_mean = sum(row[2] for row in stat) * (1.0 / width)
    cross = sum(row[3] + (row[0] - mean) * row[2] for row in stat) * inverse * (1.0 / width)

    for chip in range(CHIPS):
        where = slice(chip * ROWS, (chip + 1) * ROWS)
        up = mine_ref[chip, 3].astype(F32).T
        hat = (att_ref[:, where] - mean[:, where]) * inverse[:, where]
        out_ref[chip, 3] = hat.T.astype(BF16)
        grad = inverse[:, where] * (up - up_mean[:, where] - hat * cross[:, where])
        grad_t_ref[:, where] = grad.astype(BF16)
        grad_ref[where, :] = grad.T.astype(BF16)
        query_t_ref[:, where] = mine_ref[chip, 2].T
    for block in range(GROUP):
        where = slice(block * ROWS, (block + 1) * ROWS)
        key_t_ref[:, where] = key_ref[where, :].T

    def pair(j, m):
        keys = slice(key_tile * j, key_tile * (j + 1))
        rows = slice(m * ROWS, (m + 1) * ROWS)
        half_scores = dot(key_ref[keys, :], query_t_ref[:, rows]) * scale
        grad_weights = dot(value_ref[keys, :], grad_t_ref[:, rows])
        plus = jnp.tanh(half_scores) + 1.0
        weights = half_scores * plus
        grad_scores = grad_weights * (plus * ((half_scores + half_scores + 1.0) - weights))
        if m == j:
            query_spot = lax.broadcasted_iota(jnp.int32, (key_tile, ROWS), 1) + core * ROWS
            key_spot = lax.broadcasted_iota(jnp.int32, (key_tile, ROWS), 0)
            allowed = key_spot <= query_spot
            weights = jnp.where(allowed, weights, 0.0)
            grad_scores = jnp.where(allowed, grad_scores, 0.0)
        weights = weights.astype(BF16)
        grad_scores = grad_scores.astype(BF16)
        dv = dot(weights, grad_ref[rows, :])
        dk = dot(grad_scores, mine_ref[m, 2])
        dq = dot(key_t_ref[:, keys], grad_scores)
        if m == j:
            dv_ref[keys, :] = dv
            dk_ref[keys, :] = dk
        else:
            dv_ref[keys, :] += dv
            dk_ref[keys, :] += dk
        if j == 0:
            dq_ref[:, rows] = dq
        else:
            dq_ref[:, rows] += dq

    for j in range(CHIPS):

        @pl.when(key_tile * j < length)
        def _():
            for m in range(j, CHIPS):
                pair(j, m)

        @pl.when(key_tile * j >= length)
        def _():
            keys = slice(key_tile * j, key_tile * (j + 1))
            dv_ref[keys, :] = jnp.zeros((key_tile, HEAD_DIM), F32)
            dk_ref[keys, :] = jnp.zeros((key_tile, HEAD_DIM), F32)

    for chip in range(CHIPS):
        out_ref[chip, 2] = (dq_ref[:, chip * ROWS : (chip + 1) * ROWS].T * scale).astype(BF16)
        kept = pl.ds(pl.multiple_of((2 * chip + core) * ROWS, ROWS), ROWS)
        sent = pl.ds(pl.multiple_of((2 * chip + 1 - core) * ROWS, ROWS), ROWS)
        out_ref[chip, 0] = (dk_ref[kept, :] * scale).astype(BF16)
        out_ref[chip, 1] = dv_ref[kept, :].astype(BF16)
        sib_ref[chip, 0] = (dk_ref[sent, :] * scale).astype(BF16)
        sib_ref[chip, 1] = dv_ref[sent, :].astype(BF16)


def backward(info, mine, other, att, stats):
    half = CHIPS * ROWS
    return pl.pallas_call(
        backward_kernel,
        out_shape=[
            jax.ShapeDtypeStruct((CHIPS, 4, ROWS, HEAD_DIM), BF16),
            jax.ShapeDtypeStruct((CHIPS, 2, ROWS, HEAD_DIM), BF16),
        ],
        in_specs=[sspec(), vspec(), vspec(), vspec(), vspec()],
        out_specs=[vspec(), vspec()],
        scratch_shapes=[
            VMEM((2 * half, HEAD_DIM), BF16),
            VMEM((HEAD_DIM, 2 * half), BF16),
            VMEM((2 * half, HEAD_DIM), BF16),
            VMEM((HEAD_DIM, half), BF16),
            VMEM((half, HEAD_DIM), BF16),
            VMEM((HEAD_DIM, half), BF16),
            VMEM((HEAD_DIM, half), F32),
            VMEM((2 * half, HEAD_DIM), F32),
            VMEM((2 * half, HEAD_DIM), F32),
        ],
        compiler_params=params(),
        name="backward",
    )(info, mine, other, att, stats)


def merge_kernel(out_ref, sib_ref, done_ref):
    done_ref[:, 0:2] = (out_ref[:, 0:2].astype(F32) + sib_ref[...].astype(F32)).astype(BF16)
    done_ref[:, 2:4] = out_ref[:, 2:4]


def merge(out, sib):
    return pl.pallas_call(
        merge_kernel,
        out_shape=jax.ShapeDtypeStruct(out.shape, out.dtype),
        in_specs=[vspec(), vspec()],
        out_specs=vspec(),
        compiler_params=params(16 * 1024 * 1024),
        name="merge",
    )(out, sib)


def finish_kernel(
    back_ref,
    gate_ref,
    slope_ref,
    hist_ref,
    up_ref,
    cot_ref,
    place_ref,
    w_in_ref,
    w_out_ref,
    mixed_ref,
    rows_ref,
    part_ref,
    total_ref,
):
    step = pl.program_id(0)

    def gather(part):
        for head in range(HEADS):
            part_ref[:, head * HEAD_DIM : (head + 1) * HEAD_DIM] = back_ref[head, part]
        return part_ref[...].astype(F32)

    def add(grad):
        pre = (grad * slope_ref[...].astype(F32)).astype(BF16)
        return dot_nt(pre, w_in_ref[...])

    @pl.when(step == 0)
    def _():
        hat = gather(3)
        gated = (hat * gate_ref[...].astype(F32)).astype(BF16)
        mixed_ref[...] = (hist_ref[...].astype(F32) + dot(gated, w_out_ref[...])).astype(BF16)
        total_ref[...] = add(up_ref[...] * hat)

    for s, part in ((1, 1), (2, 2), (3, 0)):

        @pl.when(step == s)
        def _():
            total_ref[...] += add(gather(part))

    @pl.when(step == 3)
    def _():
        hat, inverse = normalize(hist_ref[...].astype(F32))
        grad = total_ref[...]
        grad = inverse * (grad - row_mean(grad) - hat * row_mean(grad * hat))
        grad = (grad + cot_ref[...].astype(F32)).astype(BF16)
        rows_ref[...] = dot(onehot(place_ref[...]), grad).astype(BF16)


def finish(back, gate, slope, history, upstream, cotangent, place, w_in, w_out):
    rows, width = history.shape

    def whole(*shape):
        return pl.BlockSpec(shape, lambda j, *_: (0,) * len(shape))

    return pl.pallas_call(
        finish_kernel,
        grid_spec=pltpu.PrefetchScalarGridSpec(
            num_scalar_prefetch=0,
            grid=(4,),
            in_specs=[
                whole(CHIPS, 4, ROWS, HEAD_DIM),
                whole(rows, width),
                pl.BlockSpec((rows, width), lambda j, *_: (0, j)),
                whole(rows, width),
                whole(rows, width),
                whole(rows, width),
                whole(1, rows),
                pl.BlockSpec((width, width), lambda j, *_: (0, j)),
                whole(width, width),
            ],
            out_specs=[whole(rows, width), whole(rows, width)],
            scratch_shapes=[VMEM((rows, width), BF16), VMEM((rows, width), F32)],
        ),
        out_shape=[
            jax.ShapeDtypeStruct((rows, width), BF16),
            jax.ShapeDtypeStruct((rows, width), BF16),
        ],
        compiler_params=params(),
        name="finish",
    )(back, gate, slope, history, upstream, cotangent, place, w_in, w_out)


def body(log_rows, send_order, place, hist_len, w_in, w_out, cotangent):
    rows, width = log_rows.shape
    seq_size = lax.axis_size("seq")
    seq_index = lax.axis_index("seq")
    spot = seq_index % GROUP
    length = jnp.take(hist_len[0], seq_index // GROUP)
    info = jnp.stack([length, spot, spot % 2]).astype(jnp.int32)
    same_core = [list(range(g + c, g + GROUP, 2)) for g in range(0, seq_size, GROUP) for c in (0, 1)]
    swap = [(i, i ^ 1) for i in range(seq_size)]

    def to_all(block):
        block = block.reshape(rows // 2, 2, width)
        block = lax.all_to_all(block, ("dp", "seq"), split_axis=0, concat_axis=0, tiled=True)
        return block.reshape(rows, width)

    def to_group(block, members):
        return lax.all_to_all(
            block, "seq", split_axis=0, concat_axis=0, tiled=True, axis_index_groups=members
        )

    upstream = jnp.dot(cotangent, w_out.T, preferred_element_type=F32)
    arrived = to_all(pick_rows(log_rows, send_order))
    history, gate, slope, block = project(arrived, place, w_in, upstream)
    mine = to_group(block, same_core)
    other = lax.ppermute(mine[:, :2], "seq", swap)
    att, stats = forward(info, mine, other)
    stats = to_group(stats, same_core)
    out, sib = backward(info, mine, other, att, stats)
    sib = lax.ppermute(sib, "seq", swap)
    back = to_group(merge(out, sib), same_core)
    mixed, grads = finish(
        back, gate, slope, history, upstream, cotangent, place, w_in, w_out
    )
    log_grad = unpick_rows(to_all(grads), send_order, F32)
    return (mixed, log_grad)


def solution(mesh):
    rows = P(("dp", "seq"), None)
    return jax.shard_map(
        body,
        mesh=mesh,
        in_specs=(rows, rows, rows, P("dp", None), P(), P(), rows),
        out_specs=(rows, rows),
        check_vma=False,
    )
```

```python
import functools
import math

import jax
import jax.numpy as jnp
from jax import lax
from jax.experimental import pallas as pl
from jax.experimental.pallas import tpu as pltpu
from jax.sharding import PartitionSpec as P

HEADS = 8
GROUP = 16
EPSILON = 1e-05
CHIPS = 8
ROWS = 256
HEAD_DIM = 128
MIB = 1024 * 1024
DENSE = 56
SMALL = 48
ATTN = 48
BF16 = jnp.bfloat16
F32 = jnp.float32
VMEM = pltpu.VMEM
SMEM = pltpu.SMEM


def params(mib):
    return pltpu.CompilerParams(vmem_limit_bytes=mib * MIB)


def vspec():
    return pl.BlockSpec(memory_space=VMEM)


def aspec():
    return pl.BlockSpec(memory_space=pl.ANY)


def hspec():
    return pl.BlockSpec(memory_space=pltpu.HBM)


def sspec():
    return pl.BlockSpec(memory_space=SMEM)


def dot(a, b):
    return jnp.dot(a, b, preferred_element_type=F32)


def dot_nt(a, b):
    return lax.dot_general(a, b, (((1,), (1,)), ((), ())), preferred_element_type=F32)


def dot_tn(a, b):
    return lax.dot_general(a, b, (((0,), (0,)), ((), ())), preferred_element_type=F32)


def onehot(order):
    count = order.shape[1]
    spots = lax.broadcasted_iota(jnp.int32, (count, count), 0)
    return jnp.where(spots == order, 1.0, 0.0).astype(BF16)


def row_mean(x):
    return jnp.mean(x, axis=-1, keepdims=True)


def normalize(inputs):
    centred = inputs - row_mean(inputs)
    inverse = lax.rsqrt(row_mean(centred * centred) + EPSILON)
    return centred * inverse, inverse


def pick_kernel(rows_ref, order_ref, out_ref):
    rows = dot_tn(onehot(order_ref[...]), rows_ref[...]).astype(out_ref.dtype)
    out_ref[...] = rows.reshape(out_ref.shape)


def pick_rows(rows, order):
    return pl.pallas_call(
        pick_kernel,
        out_shape=jax.ShapeDtypeStruct((rows.shape[0] // 2, 2, rows.shape[1]), rows.dtype),
        in_specs=[vspec(), vspec()],
        out_specs=vspec(),
        compiler_params=params(SMALL),
        name="pick_rows",
    )(rows, order)


def unpick_kernel(rows_ref, order_ref, out_ref):
    out_ref[...] = dot(onehot(order_ref[...]), rows_ref[...].reshape(out_ref.shape)).astype(
        out_ref.dtype
    )


def unpick_rows(rows, order, dtype):
    return pl.pallas_call(
        unpick_kernel,
        out_shape=jax.ShapeDtypeStruct((2 * rows.shape[0], rows.shape[2]), dtype),
        in_specs=[vspec(), vspec()],
        out_specs=vspec(),
        compiler_params=params(SMALL),
        name="unpick_rows",
    )(rows, order)


CHUNK = 512


def start_weights(w_hbm, w_ref, sems, blocks):
    width = w_hbm.shape[0]
    per = width // CHUNK

    def copy(slot, chunk):
        return pltpu.make_async_copy(
            w_hbm.at[:, pl.ds(blocks[slot] * width + chunk * CHUNK, CHUNK)],
            w_ref.at[slot * per + chunk],
            sems.at[slot * per + chunk],
        )

    for slot in range(len(blocks)):
        for chunk in range(per):
            copy(slot, chunk).start()
    return lambda slot, chunk: copy(slot, chunk).wait()


def chunks(width):
    return [(c, slice(c * CHUNK, (c + 1) * CHUNK)) for c in range(width // CHUNK)]


def activate(preact):
    sigmoid = jnp.tanh(preact * 0.5) * 0.5 + 0.5
    act = preact * sigmoid
    return act.astype(BF16), (sigmoid + act - act * sigmoid).astype(BF16)


def lay(buf_ref, part, chunk, block):
    heads = CHUNK // HEAD_DIM
    for head in range(heads):
        buf_ref[chunk * heads + head, part] = block[:, head * HEAD_DIM : (head + 1) * HEAD_DIM]


def project_kq_kernel(
    info,
    arrived_ref,
    place_ref,
    w_hbm,
    _,
    hist_ref,
    normed_ref,
    slope_ref,
    buf_ref,
    w_ref,
    sems,
):
    rows, width = hist_ref.shape
    arrive = start_weights(w_hbm, w_ref, sems, (3, 2))
    history = dot_tn(onehot(place_ref[...]), arrived_ref[...].reshape(rows, width))
    hist_ref[...] = history.astype(BF16)
    normed = normalize(history)[0].astype(BF16)
    normed_ref[...] = normed
    for part in range(2):
        for chunk, columns in chunks(width):
            arrive(part, chunk)
            act, slope = activate(dot(normed, w_ref[part * (width // CHUNK) + chunk]))
            slope_ref[part, :, columns] = slope
            lay(buf_ref, part, chunk, act)


def project_vu_kernel(
    normed_ref, w_hbm, up_ref, gate_ref, slope_ref, buf_ref, token_ref, w_ref, sems
):
    width = normed_ref.shape[1]
    arrive = start_weights(w_hbm, w_ref, sems, (1, 0))
    normed = normed_ref[...]
    for part in range(2):
        for chunk, columns in chunks(width):
            arrive(part, chunk)
            act, slope = activate(dot(normed, w_ref[part * (width // CHUNK) + chunk]))
            slope_ref[part, :, columns] = slope
            if part:
                gate_ref[:, columns] = act
                act = (up_ref[:, columns] * act.astype(F32)).astype(BF16)
            lay(buf_ref, part, chunk, act)
    token_ref[...] = jnp.zeros_like(token_ref)


def weight_scratch(width):
    count = 2 * (width // CHUNK)
    return [VMEM((count, width, CHUNK), BF16), pltpu.SemaphoreType.DMA((count,))]


def dense_cost(rows, width, blocks):
    return pl.CostEstimate(
        flops=2 * rows * width * width * blocks,
        bytes_accessed=2 * width * width * blocks + 8 * rows * width * blocks,
        transcendentals=rows * width * blocks,
    )


def project_kq(info, arrived, place, w_in, upstream):
    rows, width = upstream.shape
    return pl.pallas_call(
        project_kq_kernel,
        in_specs=[sspec(), vspec(), vspec(), hspec(), aspec()],
        out_specs=[vspec()] * 4,
        out_shape=[
            jax.ShapeDtypeStruct((rows, width), BF16),
            jax.ShapeDtypeStruct((rows, width), BF16),
            jax.ShapeDtypeStruct((2, rows, width), BF16),
            jax.ShapeDtypeStruct((CHIPS, 2, ROWS, HEAD_DIM), BF16),
        ],
        scratch_shapes=weight_scratch(width),
        compiler_params=params(DENSE),
        cost_estimate=dense_cost(rows, width, 2),
        name="project_kq",
    )(info, arrived, place, w_in, upstream)


def project_vu(normed, w_in, upstream):
    rows, width = normed.shape
    return pl.pallas_call(
        project_vu_kernel,
        in_specs=[vspec(), hspec(), vspec()],
        out_specs=[vspec()] * 4,
        out_shape=[
            jax.ShapeDtypeStruct((rows, width), BF16),
            jax.ShapeDtypeStruct((2, rows, width), BF16),
            jax.ShapeDtypeStruct((CHIPS, 2, ROWS, HEAD_DIM), BF16),
            jax.ShapeDtypeStruct((8, HEAD_DIM), F32),
        ],
        scratch_shapes=weight_scratch(width),
        compiler_params=params(DENSE),
        cost_estimate=dense_cost(rows, width, 2),
        name="project_vu",
    )(normed, w_in, upstream)


def part_kernel(pair_ref, _, out_ref):
    out_ref[...] = pair_ref[:, 0]


def first_part(pair, after):
    chips, _, rows, width = pair.shape
    return pl.pallas_call(
        part_kernel,
        out_shape=jax.ShapeDtypeStruct((chips, rows, width), pair.dtype),
        in_specs=[vspec(), aspec()],
        out_specs=vspec(),
        compiler_params=params(SMALL),
        name="first_part",
    )(pair, after)


TILES = CHIPS * (CHIPS + 1) // 2
KEY_TILE = 2 * ROWS
SCALE = 0.5 / math.sqrt(HEAD_DIM)


def tile_of(j, m):
    return j * CHIPS - j * (j - 1) // 2 + m - j


def lay_rows(info, own_ref, other_ref, out_ref):
    length, core = info[0], info[1]
    for chip in range(CHIPS):
        for source, side in ((own_ref.at[chip, 0], core), (other_ref.at[chip], 1 - core)):
            start = pl.multiple_of((2 * chip + side) * ROWS, ROWS)
            out_ref[pl.ds(start, ROWS), :] = source[...]

    @pl.when(length < GROUP * ROWS)
    def _():
        def clear(block, carry):
            where = pl.ds(pl.multiple_of(block * ROWS, ROWS), ROWS)
            spots = lax.broadcasted_iota(jnp.int32, (ROWS, HEAD_DIM), 0) + block * ROWS
            rows = jnp.where(spots < length, out_ref[where, :].astype(F32), 0.0)
            out_ref[where, :] = rows.astype(BF16)
            return carry

        lax.fori_loop(length // ROWS, GROUP, clear, 0)


def each_tile(length, work, dead=None, order=range(CHIPS)[::-1]):
    for j in order:
        if j == 0:
            work(0)
            continue
        pl.when(KEY_TILE * j < length)(functools.partial(work, j))
        if dead is not None:
            pl.when(KEY_TILE * j >= length)(functools.partial(dead, j))


def tiles_of(j):
    return pl.ds(tile_of(j, j), CHIPS - j)


def fetch_tiles(length, kept_ref, here_ref, sems):
    def copy(j):
        return pltpu.make_async_copy(kept_ref.at[tiles_of(j)], here_ref.at[tiles_of(j)], sems.at[j])

    each_tile(length, lambda j: copy(j).start())
    return lambda j: copy(j).wait()


def keys_of(j):
    return slice(KEY_TILE * j, KEY_TILE * (j + 1))


def rows_of(m):
    return slice(ROWS * m, ROWS * (m + 1))


def weigh_kernel(
    info,
    kq_ref,
    other_ref,
    _,
    weight_out,
    slope_out,
    token_ref,
    key_ref,
    query_t_ref,
    weight_ref,
    slope_ref,
    weight_sems,
    slope_sems,
):
    length, core = info[0], info[1]

    def copies(j):
        where = tiles_of(j)
        return (
            pltpu.make_async_copy(weight_ref.at[where], weight_out.at[where], weight_sems.at[j]),
            pltpu.make_async_copy(slope_ref.at[where], slope_out.at[where], slope_sems.at[j]),
        )

    lay_rows(info, kq_ref, other_ref, key_ref)
    for m in range(CHIPS):
        query_t_ref[:, rows_of(m)] = (kq_ref[m, 1].astype(F32) * SCALE).T.astype(BF16)

    def work(j):
        for m in range(j, CHIPS):
            half = dot(key_ref[keys_of(j), :], query_t_ref[:, rows_of(m)])
            tanh = jnp.tanh(half)
            weights = half * (1.0 + tanh)
            slope = (1.0 + tanh) + weights * (1.0 - tanh)
            if m == j:
                query_spot = lax.broadcasted_iota(jnp.int32, (KEY_TILE, ROWS), 1) + core * ROWS
                key_spot = lax.broadcasted_iota(jnp.int32, (KEY_TILE, ROWS), 0)
                allowed = key_spot <= query_spot
                weights = jnp.where(allowed, weights, 0.0)
                slope = jnp.where(allowed, slope, 0.0)
            weight_ref[tile_of(j, m)] = weights.astype(BF16)
            slope_ref[tile_of(j, m)] = slope.astype(BF16)
        for copy in copies(j):
            copy.start()

    def drain(j):
        for copy in copies(j):
            copy.wait()

    each_tile(length, work, order=range(CHIPS))
    token_ref[...] = jnp.zeros_like(token_ref)
    each_tile(length, drain)


def attention_cost(matmuls, exps):
    area = TILES * KEY_TILE * ROWS
    return pl.CostEstimate(
        flops=4 * matmuls * area * HEAD_DIM, bytes_accessed=4 * area, transcendentals=exps * area
    )


def weigh(info, kq, other, after):
    half = CHIPS * ROWS
    return pl.pallas_call(
        weigh_kernel,
        out_shape=[
            jax.ShapeDtypeStruct((TILES, KEY_TILE, ROWS), BF16),
            jax.ShapeDtypeStruct((TILES, KEY_TILE, ROWS), BF16),
            jax.ShapeDtypeStruct((8, HEAD_DIM), F32),
        ],
        in_specs=[sspec(), vspec(), vspec(), aspec()],
        out_specs=[hspec(), hspec(), vspec()],
        scratch_shapes=[
            VMEM((2 * half, HEAD_DIM), BF16),
            VMEM((HEAD_DIM, half), BF16),
            VMEM((TILES, KEY_TILE, ROWS), BF16),
            VMEM((TILES, KEY_TILE, ROWS), BF16),
            pltpu.SemaphoreType.DMA((CHIPS,)),
            pltpu.SemaphoreType.DMA((CHIPS,)),
        ],
        compiler_params=params(ATTN),
        cost_estimate=attention_cost(1, 1),
        name="weigh",
    )(info, kq, other, after)


def attend_kernel(
    info,
    vu_ref,
    other_ref,
    weight_hbm,
    att_ref,
    stats_ref,
    value_ref,
    value_t_ref,
    weight_ref,
    sems,
):
    length = info[0]
    arrive = fetch_tiles(length, weight_hbm, weight_ref, sems)
    lay_rows(info, vu_ref, other_ref, value_ref)
    att_ref[...] = jnp.zeros_like(att_ref)

    def work(j):
        arrive(j)
        for block in (2 * j, 2 * j + 1):
            value_t_ref[:, rows_of(block)] = value_ref[rows_of(block), :].T
        for m in range(j, CHIPS):
            att_ref[:, rows_of(m)] += dot(value_t_ref[:, keys_of(j)], weight_ref[tile_of(j, m)])

    each_tile(length, work)
    for m in range(CHIPS):
        att = att_ref[:, rows_of(m)]
        up = vu_ref[m, 1].astype(F32).T
        mean = jnp.mean(att, axis=0, keepdims=True)
        centred = att - mean
        stats = jnp.concatenate(
            [
                mean,
                jnp.sum(centred * centred, axis=0, keepdims=True),
                jnp.sum(up, axis=0, keepdims=True),
                jnp.sum(up * centred, axis=0, keepdims=True),
            ],
            axis=0,
        )
        for head in range(HEADS):
            stats_ref[head, :, rows_of(m)] = stats


def attend(info, vu, other, weights):
    half = CHIPS * ROWS
    return pl.pallas_call(
        attend_kernel,
        out_shape=[
            jax.ShapeDtypeStruct((HEAD_DIM, half), F32),
            jax.ShapeDtypeStruct((HEADS, 4, half), F32),
        ],
        in_specs=[sspec(), vspec(), vspec(), hspec()],
        out_specs=[vspec(), vspec()],
        scratch_shapes=[
            VMEM((2 * half, HEAD_DIM), BF16),
            VMEM((HEAD_DIM, 2 * half), BF16),
            VMEM((TILES, KEY_TILE, ROWS), BF16),
            pltpu.SemaphoreType.DMA((CHIPS,)),
        ],
        compiler_params=params(ATTN),
        cost_estimate=attention_cost(1, 0),
        name="attend",
    )(info, vu, other, weights)


def back_v_kernel(
    info,
    vu_ref,
    att_ref,
    stats_ref,
    weight_hbm,
    out_ref,
    sib_ref,
    grad_t_ref,
    grad_ref,
    dv_ref,
    weight_ref,
    sems,
):
    length, core = info[0], info[1]
    arrive = fetch_tiles(length, weight_hbm, weight_ref, sems)
    width = HEADS * HEAD_DIM
    stat = [[stats_ref[head, s : s + 1, :] for s in range(4)] for head in range(HEADS)]
    mean = sum(row[0] for row in stat) * (1.0 / HEADS)
    square = sum(row[1] + HEAD_DIM * (row[0] - mean) * (row[0] - mean) for row in stat)
    inverse = lax.rsqrt(square * (1.0 / width) + EPSILON)
    up_mean = sum(row[2] for row in stat) * (1.0 / width)
    cross = sum(row[3] + (row[0] - mean) * row[2] for row in stat) * inverse * (1.0 / width)
    for m in range(CHIPS):
        where = rows_of(m)
        up = vu_ref[m, 1].astype(F32).T
        hat = (att_ref[:, where] - mean[:, where]) * inverse[:, where]
        out_ref[m, 1] = hat.T.astype(BF16)
        grad = inverse[:, where] * (up - up_mean[:, where] - hat * cross[:, where])
        grad_t_ref[:, where] = grad.astype(BF16)
        grad_ref[where, :] = grad.T.astype(BF16)

    def work(j):
        arrive(j)
        for m in range(j, CHIPS):
            term = dot(weight_ref[tile_of(j, m)], grad_ref[rows_of(m), :])
            if m == j:
                dv_ref[keys_of(j), :] = term
            else:
                dv_ref[keys_of(j), :] += term

    def dead(j):
        dv_ref[keys_of(j), :] = jnp.zeros((KEY_TILE, HEAD_DIM), F32)

    each_tile(length, work, dead)
    share(core, dv_ref, 1.0, out_ref, sib_ref)


def share(core, sum_ref, scale, out_ref, sib_ref):
    for chip in range(CHIPS):
        kept = pl.ds(pl.multiple_of((2 * chip + core) * ROWS, ROWS), ROWS)
        sent = pl.ds(pl.multiple_of((2 * chip + 1 - core) * ROWS, ROWS), ROWS)
        out_ref[chip, 0] = (sum_ref[kept, :] * scale).astype(BF16)
        sib_ref[chip] = (sum_ref[sent, :] * scale).astype(BF16)


def back_v(info, vu, att, stats, weights):
    half = CHIPS * ROWS
    return pl.pallas_call(
        back_v_kernel,
        out_shape=[
            jax.ShapeDtypeStruct((CHIPS, 2, ROWS, HEAD_DIM), BF16),
            jax.ShapeDtypeStruct((CHIPS, ROWS, HEAD_DIM), BF16),
            jax.ShapeDtypeStruct((HEAD_DIM, half), BF16),
        ],
        in_specs=[sspec(), vspec(), vspec(), vspec(), hspec()],
        out_specs=[vspec(), vspec(), vspec()],
        scratch_shapes=[
            VMEM((half, HEAD_DIM), BF16),
            VMEM((2 * half, HEAD_DIM), F32),
            VMEM((TILES, KEY_TILE, ROWS), BF16),
            pltpu.SemaphoreType.DMA((CHIPS,)),
        ],
        compiler_params=params(ATTN),
        cost_estimate=attention_cost(1, 0),
        name="back_v",
    )(info, vu, att, stats, weights)


def back_kq_kernel(
    info,
    kq_ref,
    vu_ref,
    other_ref,
    other_key_ref,
    slope_hbm,
    grad_t_ref,
    out_ref,
    sib_ref,
    value_ref,
    key_t_ref,
    dq_ref,
    dk_ref,
    slope_ref,
    sems,
):
    length, core = info[0], info[1]
    arrive = fetch_tiles(length, slope_hbm, slope_ref, sems)
    lay_rows(info, vu_ref, other_ref, value_ref)
    dq_ref[...] = jnp.zeros_like(dq_ref)
    for chip in range(CHIPS):
        for rows, side in ((kq_ref[chip, 0], core), (other_key_ref[chip], 1 - core)):
            start = pl.multiple_of((2 * chip + side) * ROWS, ROWS)
            key_t_ref[:, pl.ds(start, ROWS)] = rows.T

    def work(j):
        arrive(j)
        for m in range(j, CHIPS):
            grad = dot(value_ref[keys_of(j), :], grad_t_ref[:, rows_of(m)])
            grad = (grad * slope_ref[tile_of(j, m)].astype(F32)).astype(BF16)
            dk = dot(grad, kq_ref[m, 1])
            dq = dot(key_t_ref[:, keys_of(j)], grad)
            if m == j:
                dk_ref[keys_of(j), :] = dk
            else:
                dk_ref[keys_of(j), :] += dk
            dq_ref[:, rows_of(m)] += dq

    def dead(j):
        dk_ref[keys_of(j), :] = jnp.zeros((KEY_TILE, HEAD_DIM), F32)

    each_tile(length, work, dead)
    for m in range(CHIPS):
        out_ref[m, 1] = (dq_ref[:, rows_of(m)].T * SCALE).astype(BF16)
    share(core, dk_ref, SCALE, out_ref, sib_ref)


def back_kq(info, kq, vu, other, other_keys, slope, grad_t):
    half = CHIPS * ROWS
    return pl.pallas_call(
        back_kq_kernel,
        out_shape=[
            jax.ShapeDtypeStruct((CHIPS, 2, ROWS, HEAD_DIM), BF16),
            jax.ShapeDtypeStruct((CHIPS, ROWS, HEAD_DIM), BF16),
        ],
        in_specs=[sspec()] + [vspec()] * 4 + [hspec(), vspec()],
        out_specs=[vspec(), vspec()],
        scratch_shapes=[
            VMEM((2 * half, HEAD_DIM), BF16),
            VMEM((HEAD_DIM, 2 * half), BF16),
            VMEM((HEAD_DIM, half), F32),
            VMEM((2 * half, HEAD_DIM), F32),
            VMEM((TILES, KEY_TILE, ROWS), BF16),
            pltpu.SemaphoreType.DMA((CHIPS,)),
        ],
        compiler_params=params(ATTN),
        cost_estimate=attention_cost(3, 0),
        name="back_kq",
    )(info, kq, vu, other, other_keys, slope, grad_t)


def merge_kernel(out_ref, sib_ref, done_ref):
    done_ref[:, 0] = (out_ref[:, 0].astype(F32) + sib_ref[...].astype(F32)).astype(BF16)
    done_ref[:, 1] = out_ref[:, 1]


def merge(out, sib):
    return pl.pallas_call(
        merge_kernel,
        out_shape=jax.ShapeDtypeStruct(out.shape, out.dtype),
        in_specs=[vspec(), vspec()],
        out_specs=vspec(),
        compiler_params=params(SMALL),
        name="merge",
    )(out, sib)


def gather(back_ref, part, chunk):
    heads = CHUNK // HEAD_DIM
    blocks = [back_ref[chunk * heads + head, part].astype(F32) for head in range(heads)]
    return jnp.concatenate(blocks, axis=1)


def finish_vg_kernel(
    back_ref,
    gate_ref,
    slope_ref,
    hist_ref,
    up_ref,
    w_hbm,
    w_out_ref,
    mixed_ref,
    sum_ref,
    w_ref,
    sems,
):
    width = hist_ref.shape[1]
    arrive = start_weights(w_hbm, w_ref, sems, (1, 0))
    mixed = hist_ref[...].astype(F32)
    total = jnp.zeros(hist_ref.shape, F32)
    for part in range(2):
        for chunk, columns in chunks(width):
            grad = gather(back_ref, part, chunk)
            if part:
                gated = (grad * gate_ref[:, columns].astype(F32)).astype(BF16)
                mixed = mixed + dot(gated, w_out_ref[columns, :])
                grad = grad * up_ref[:, columns]
            pre = (grad * slope_ref[part, :, columns].astype(F32)).astype(BF16)
            arrive(part, chunk)
            total = total + dot_nt(pre, w_ref[part * (width // CHUNK) + chunk])
    mixed_ref[...] = mixed.astype(BF16)
    sum_ref[...] = total


def finish_vg(back, gate, slope, history, upstream, w_in, w_out):
    rows, width = history.shape
    return pl.pallas_call(
        finish_vg_kernel,
        in_specs=[vspec()] * 5 + [hspec(), vspec()],
        out_specs=[vspec(), vspec()],
        scratch_shapes=weight_scratch(width),
        out_shape=[
            jax.ShapeDtypeStruct((rows, width), BF16),
            jax.ShapeDtypeStruct((rows, width), F32),
        ],
        compiler_params=params(DENSE),
        cost_estimate=dense_cost(rows, width, 3),
        name="finish_vg",
    )(back, gate, slope, history, upstream, w_in, w_out)


def finish_kq_kernel(
    back_ref, slope_ref, hist_ref, start_ref, cot_ref, place_ref, w_hbm, rows_ref, w_ref, sems
):
    width = hist_ref.shape[1]
    arrive = start_weights(w_hbm, w_ref, sems, (3, 2))
    hat, inverse = normalize(hist_ref[...].astype(F32))
    grad = start_ref[...]
    for part in range(2):
        for chunk, columns in chunks(width):
            pre = gather(back_ref, part, chunk) * slope_ref[part, :, columns].astype(F32)
            arrive(part, chunk)
            grad = grad + dot_nt(pre.astype(BF16), w_ref[part * (width // CHUNK) + chunk])
    grad = inverse * (grad - row_mean(grad) - hat * row_mean(grad * hat))
    grad = (grad + cot_ref[...].astype(F32)).astype(BF16)
    rows_ref[...] = dot(onehot(place_ref[...]), grad).astype(BF16).reshape(rows_ref.shape)


def finish_kq(back, slope, history, start, cotangent, place, w_in):
    rows, width = history.shape
    return pl.pallas_call(
        finish_kq_kernel,
        in_specs=[vspec()] * 6 + [hspec()],
        out_specs=vspec(),
        scratch_shapes=weight_scratch(width),
        out_shape=jax.ShapeDtypeStruct((rows // 2, 2, width), BF16),
        compiler_params=params(DENSE),
        cost_estimate=dense_cost(rows, width, 2),
        name="finish_kq",
    )(back, slope, history, start, cotangent, place, w_in)


def body(log_rows, send_order, place, hist_len, w_in, w_out, cotangent):
    seq_size = lax.axis_size("seq")
    seq_index = lax.axis_index("seq")
    spot = seq_index % GROUP
    length = jnp.take(hist_len[0], seq_index // GROUP)
    info = jnp.stack([length, spot % 2]).astype(jnp.int32)
    same_core = [list(range(g + c, g + GROUP, 2)) for g in range(0, seq_size, GROUP) for c in (0, 1)]
    swap = [(i, i ^ 1) for i in range(seq_size)]

    def to_all(block):
        return lax.all_to_all(block, ("dp", "seq"), split_axis=0, concat_axis=0, tiled=True)

    def to_group(block, members):
        return lax.all_to_all(
            block, "seq", split_axis=0, concat_axis=0, tiled=True, axis_index_groups=members
        )

    upstream = jnp.dot(cotangent, w_out.T, preferred_element_type=F32)
    arrived = to_all(pick_rows(log_rows, send_order))
    history, normed, slope_kq, kq = project_kq(info, arrived, place, w_in, upstream)
    kq = to_group(kq, same_core)
    gate, slope_vg, vu, token = project_vu(normed, w_in, upstream)
    other_keys = lax.ppermute(first_part(kq, token), "seq", swap)
    weights, slopes, token = weigh(info, kq, other_keys, token)
    vu = to_group(vu, same_core)
    other_values = lax.ppermute(first_part(vu, token), "seq", swap)
    att, stats = attend(info, vu, other_values, weights)
    stats = to_group(stats, same_core)
    out, sib, grad_t = back_v(info, vu, att, stats, weights)
    back_vh = merge(out, lax.ppermute(sib, "seq", swap))
    out, sib = back_kq(info, kq, vu, other_values, other_keys, slopes, grad_t)
    back_vh = to_group(back_vh, same_core)
    back_kq_rows = merge(out, lax.ppermute(sib, "seq", swap))
    mixed, start = finish_vg(back_vh, gate, slope_vg, history, upstream, w_in, w_out)
    back_kq_rows = to_group(back_kq_rows, same_core)
    grads = finish_kq(back_kq_rows, slope_kq, history, start, cotangent, place, w_in)
    log_grad = unpick_rows(to_all(grads), send_order, F32)
    return (mixed, log_grad)


def solution(mesh):
    rows = P(("dp", "seq"), None)
    return jax.shard_map(
        body,
        mesh=mesh,
        in_specs=(rows, rows, rows, P("dp", None), P(), P(), rows),
        out_specs=(rows, rows),
        check_vma=False,
    )
```

```python
import functools
import math

import jax
import jax.numpy as jnp
from jax import lax
from jax.experimental import pallas as pl
from jax.experimental.pallas import tpu as pltpu
from jax.sharding import PartitionSpec as P

HEADS = 8
GROUP = 16
EPSILON = 1e-05
CHIPS = 8
ROWS = 256
HEAD_DIM = 128
MIB = 1024 * 1024
DENSE = 56
SMALL = 48
ATTN = 48
BF16 = jnp.bfloat16
F32 = jnp.float32
VMEM = pltpu.VMEM
SMEM = pltpu.SMEM


def params(mib):
    return pltpu.CompilerParams(vmem_limit_bytes=mib * MIB)


def vspec():
    return pl.BlockSpec(memory_space=VMEM)


def aspec():
    return pl.BlockSpec(memory_space=pl.ANY)


def hspec():
    return pl.BlockSpec(memory_space=pltpu.HBM)


def sspec():
    return pl.BlockSpec(memory_space=SMEM)


def dot(a, b):
    return jnp.dot(a, b, preferred_element_type=F32)


def dot_nt(a, b):
    return lax.dot_general(a, b, (((1,), (1,)), ((), ())), preferred_element_type=F32)


def dot_tn(a, b):
    return lax.dot_general(a, b, (((0,), (0,)), ((), ())), preferred_element_type=F32)


def onehot(order):
    count = order.shape[1]
    spots = lax.broadcasted_iota(jnp.int32, (count, count), 0)
    return jnp.where(spots == order, 1.0, 0.0).astype(BF16)


def row_mean(x):
    return jnp.mean(x, axis=-1, keepdims=True)


def normalize(inputs):
    centred = inputs - row_mean(inputs)
    inverse = lax.rsqrt(row_mean(centred * centred) + EPSILON)
    return centred * inverse, inverse


def pick_kernel(rows_ref, order_ref, out_ref):
    rows = dot_tn(onehot(order_ref[...]), rows_ref[...]).astype(out_ref.dtype)
    out_ref[...] = rows.reshape(out_ref.shape)


def pick_rows(rows, order):
    return pl.pallas_call(
        pick_kernel,
        out_shape=jax.ShapeDtypeStruct((rows.shape[0] // 2, 2, rows.shape[1]), rows.dtype),
        in_specs=[vspec(), vspec()],
        out_specs=vspec(),
        compiler_params=params(DENSE),
        name="pick_rows",
    )(rows, order)


def unpick_kernel(rows_ref, order_ref, out_ref):
    out_ref[...] = dot(onehot(order_ref[...]), rows_ref[...].reshape(out_ref.shape)).astype(
        out_ref.dtype
    )


def unpick_rows(rows, order, dtype):
    return pl.pallas_call(
        unpick_kernel,
        out_shape=jax.ShapeDtypeStruct((2 * rows.shape[0], rows.shape[2]), dtype),
        in_specs=[vspec(), vspec()],
        out_specs=vspec(),
        compiler_params=params(SMALL),
        name="unpick_rows",
    )(rows, order)


CHUNK = 512


def start_weights(w_hbm, w_ref, sems, blocks):
    width = w_hbm.shape[0]
    per = width // CHUNK

    def copy(slot, chunk):
        return pltpu.make_async_copy(
            w_hbm.at[:, pl.ds(blocks[slot] * width + chunk * CHUNK, CHUNK)],
            w_ref.at[slot * per + chunk],
            sems.at[slot * per + chunk],
        )

    for slot in range(len(blocks)):
        for chunk in range(per):
            copy(slot, chunk).start()
    return lambda slot, chunk: copy(slot, chunk).wait()


def chunks(width):
    return [(c, slice(c * CHUNK, (c + 1) * CHUNK)) for c in range(width // CHUNK)]


def activate(preact):
    sigmoid = jnp.tanh(preact * 0.5) * 0.5 + 0.5
    act = preact * sigmoid
    return act.astype(BF16), (sigmoid + act - act * sigmoid).astype(BF16)


def lay(buf_ref, part, chunk, block):
    heads = CHUNK // HEAD_DIM
    for head in range(heads):
        buf_ref[chunk * heads + head, part] = block[:, head * HEAD_DIM : (head + 1) * HEAD_DIM]


def project_kq_kernel(
    info,
    arrived_ref,
    place_ref,
    w_hbm,
    _,
    hist_ref,
    normed_ref,
    slope_ref,
    buf_ref,
    w_ref,
    sems,
):
    rows, width = hist_ref.shape
    arrive = start_weights(w_hbm, w_ref, sems, (3, 2))
    history = dot_tn(onehot(place_ref[...]), arrived_ref[...].reshape(rows, width))
    hist_ref[...] = history.astype(BF16)
    normed = normalize(history)[0].astype(BF16)
    normed_ref[...] = normed
    for part in range(2):
        for chunk, columns in chunks(width):
            arrive(part, chunk)
            act, slope = activate(dot(normed, w_ref[part * (width // CHUNK) + chunk]))
            slope_ref[part, :, columns] = slope
            lay(buf_ref, part, chunk, act)


def project_vu_kernel(
    normed_ref, w_hbm, up_ref, gate_ref, slope_ref, buf_ref, token_ref, w_ref, sems
):
    width = normed_ref.shape[1]
    arrive = start_weights(w_hbm, w_ref, sems, (1, 0))
    normed = normed_ref[...]
    for part in range(2):
        for chunk, columns in chunks(width):
            arrive(part, chunk)
            act, slope = activate(dot(normed, w_ref[part * (width // CHUNK) + chunk]))
            slope_ref[part, :, columns] = slope
            if part:
                gate_ref[:, columns] = act
                act = (up_ref[:, columns] * act.astype(F32)).astype(BF16)
            lay(buf_ref, part, chunk, act)
    token_ref[...] = jnp.zeros_like(token_ref)


def weight_scratch(width):
    count = 2 * (width // CHUNK)
    return [VMEM((count, width, CHUNK), BF16), pltpu.SemaphoreType.DMA((count,))]


def project_kq(info, arrived, place, w_in, upstream):
    rows, width = upstream.shape
    return pl.pallas_call(
        project_kq_kernel,
        in_specs=[sspec(), vspec(), vspec(), hspec(), aspec()],
        out_specs=[vspec()] * 4,
        out_shape=[
            jax.ShapeDtypeStruct((rows, width), BF16),
            jax.ShapeDtypeStruct((rows, width), BF16),
            jax.ShapeDtypeStruct((2, rows, width), BF16),
            jax.ShapeDtypeStruct((CHIPS, 2, ROWS, HEAD_DIM), BF16),
        ],
        scratch_shapes=weight_scratch(width),
        compiler_params=params(DENSE),
        name="project_kq",
    )(info, arrived, place, w_in, upstream)


def project_vu(normed, w_in, upstream):
    rows, width = normed.shape
    return pl.pallas_call(
        project_vu_kernel,
        in_specs=[vspec(), hspec(), vspec()],
        out_specs=[vspec()] * 4,
        out_shape=[
            jax.ShapeDtypeStruct((rows, width), BF16),
            jax.ShapeDtypeStruct((2, rows, width), BF16),
            jax.ShapeDtypeStruct((CHIPS, 2, ROWS, HEAD_DIM), BF16),
            jax.ShapeDtypeStruct((8, HEAD_DIM), F32),
        ],
        scratch_shapes=weight_scratch(width),
        compiler_params=params(DENSE),
        name="project_vu",
    )(normed, w_in, upstream)


def part_kernel(pair_ref, _, out_ref):
    out_ref[...] = pair_ref[:, 0]


def first_part(pair, after):
    chips, _, rows, width = pair.shape
    return pl.pallas_call(
        part_kernel,
        out_shape=jax.ShapeDtypeStruct((chips, rows, width), pair.dtype),
        in_specs=[vspec(), aspec()],
        out_specs=vspec(),
        compiler_params=params(SMALL),
        name="first_part",
    )(pair, after)


TILES = CHIPS * (CHIPS + 1) // 2
KEY_TILE = 2 * ROWS
SCALE = 0.5 / math.sqrt(HEAD_DIM)


def tile_of(j, m):
    return j * CHIPS - j * (j - 1) // 2 + m - j


def lay_rows(info, own_ref, other_ref, out_ref):
    length, core = info[0], info[1]
    for chip in range(CHIPS):
        for source, side in ((own_ref.at[chip, 0], core), (other_ref.at[chip], 1 - core)):
            start = pl.multiple_of((2 * chip + side) * ROWS, ROWS)
            out_ref[pl.ds(start, ROWS), :] = source[...]

    @pl.when(length < GROUP * ROWS)
    def _():
        def clear(block, carry):
            where = pl.ds(pl.multiple_of(block * ROWS, ROWS), ROWS)
            spots = lax.broadcasted_iota(jnp.int32, (ROWS, HEAD_DIM), 0) + block * ROWS
            rows = jnp.where(spots < length, out_ref[where, :].astype(F32), 0.0)
            out_ref[where, :] = rows.astype(BF16)
            return carry

        lax.fori_loop(length // ROWS, GROUP, clear, 0)


def each_tile(length, work, dead=None, order=range(CHIPS)[::-1]):
    for j in order:
        if j == 0:
            work(0)
            continue
        pl.when(KEY_TILE * j < length)(functools.partial(work, j))
        if dead is not None:
            pl.when(KEY_TILE * j >= length)(functools.partial(dead, j))


def tiles_of(j):
    return pl.ds(tile_of(j, j), CHIPS - j)


def fetch_tiles(length, kept_ref, here_ref, sems):
    def copy(j):
        return pltpu.make_async_copy(kept_ref.at[tiles_of(j)], here_ref.at[tiles_of(j)], sems.at[j])

    each_tile(length, lambda j: copy(j).start())
    return lambda j: copy(j).wait()


def keys_of(j):
    return slice(KEY_TILE * j, KEY_TILE * (j + 1))


def rows_of(m):
    return slice(ROWS * m, ROWS * (m + 1))


def weigh_kernel(
    info,
    kq_ref,
    other_ref,
    _,
    weight_out,
    slope_out,
    token_ref,
    key_ref,
    query_t_ref,
    weight_ref,
    slope_ref,
    weight_sems,
    slope_sems,
):
    length, core = info[0], info[1]

    def copies(j):
        where = tiles_of(j)
        return (
            pltpu.make_async_copy(weight_ref.at[where], weight_out.at[where], weight_sems.at[j]),
            pltpu.make_async_copy(slope_ref.at[where], slope_out.at[where], slope_sems.at[j]),
        )

    lay_rows(info, kq_ref, other_ref, key_ref)
    for m in range(CHIPS):
        query_t_ref[:, rows_of(m)] = (kq_ref[m, 1].astype(F32) * SCALE).T.astype(BF16)

    def work(j):
        for m in range(j, CHIPS):
            half = dot(key_ref[keys_of(j), :], query_t_ref[:, rows_of(m)])
            tanh = jnp.tanh(half)
            weights = half * (1.0 + tanh)
            slope = (1.0 + tanh) + weights * (1.0 - tanh)
            if m == j:
                query_spot = lax.broadcasted_iota(jnp.int32, (KEY_TILE, ROWS), 1) + core * ROWS
                key_spot = lax.broadcasted_iota(jnp.int32, (KEY_TILE, ROWS), 0)
                allowed = key_spot <= query_spot
                weights = jnp.where(allowed, weights, 0.0)
                slope = jnp.where(allowed, slope, 0.0)
            weight_ref[tile_of(j, m)] = weights.astype(BF16)
            slope_ref[tile_of(j, m)] = slope.astype(BF16)
        for copy in copies(j):
            copy.start()

    def drain(j):
        for copy in copies(j):
            copy.wait()

    each_tile(length, work, order=range(CHIPS))
    token_ref[...] = jnp.zeros_like(token_ref)
    each_tile(length, drain)


def attention_cost(matmuls, exps):
    area = TILES * KEY_TILE * ROWS
    return pl.CostEstimate(
        flops=4 * matmuls * area * HEAD_DIM, bytes_accessed=4 * area, transcendentals=exps * area
    )


def weigh(info, kq, other, after):
    half = CHIPS * ROWS
    return pl.pallas_call(
        weigh_kernel,
        out_shape=[
            jax.ShapeDtypeStruct((TILES, KEY_TILE, ROWS), BF16),
            jax.ShapeDtypeStruct((TILES, KEY_TILE, ROWS), BF16),
            jax.ShapeDtypeStruct((8, HEAD_DIM), F32),
        ],
        in_specs=[sspec(), vspec(), vspec(), aspec()],
        out_specs=[hspec(), hspec(), vspec()],
        scratch_shapes=[
            VMEM((2 * half, HEAD_DIM), BF16),
            VMEM((HEAD_DIM, half), BF16),
            VMEM((TILES, KEY_TILE, ROWS), BF16),
            VMEM((TILES, KEY_TILE, ROWS), BF16),
            pltpu.SemaphoreType.DMA((CHIPS,)),
            pltpu.SemaphoreType.DMA((CHIPS,)),
        ],
        compiler_params=params(ATTN),
        cost_estimate=attention_cost(1, 1),
        name="weigh",
    )(info, kq, other, after)


def attend_kernel(
    info,
    vu_ref,
    other_ref,
    weight_hbm,
    att_ref,
    stats_ref,
    value_ref,
    value_t_ref,
    weight_ref,
    sems,
):
    length = info[0]
    arrive = fetch_tiles(length, weight_hbm, weight_ref, sems)
    lay_rows(info, vu_ref, other_ref, value_ref)
    att_ref[...] = jnp.zeros_like(att_ref)

    def work(j):
        arrive(j)
        for block in (2 * j, 2 * j + 1):
            value_t_ref[:, rows_of(block)] = value_ref[rows_of(block), :].T
        for m in range(j, CHIPS):
            att_ref[:, rows_of(m)] += dot(value_t_ref[:, keys_of(j)], weight_ref[tile_of(j, m)])

    each_tile(length, work)
    for m in range(CHIPS):
        att = att_ref[:, rows_of(m)]
        up = vu_ref[m, 1].astype(F32).T
        mean = jnp.mean(att, axis=0, keepdims=True)
        centred = att - mean
        stats = jnp.concatenate(
            [
                mean,
                jnp.sum(centred * centred, axis=0, keepdims=True),
                jnp.sum(up, axis=0, keepdims=True),
                jnp.sum(up * centred, axis=0, keepdims=True),
            ],
            axis=0,
        )
        for head in range(HEADS):
            stats_ref[head, :, rows_of(m)] = stats


def attend(info, vu, other, weights):
    half = CHIPS * ROWS
    return pl.pallas_call(
        attend_kernel,
        out_shape=[
            jax.ShapeDtypeStruct((HEAD_DIM, half), F32),
            jax.ShapeDtypeStruct((HEADS, 4, half), F32),
        ],
        in_specs=[sspec(), vspec(), vspec(), hspec()],
        out_specs=[vspec(), vspec()],
        scratch_shapes=[
            VMEM((2 * half, HEAD_DIM), BF16),
            VMEM((HEAD_DIM, 2 * half), BF16),
            VMEM((TILES, KEY_TILE, ROWS), BF16),
            pltpu.SemaphoreType.DMA((CHIPS,)),
        ],
        compiler_params=params(ATTN),
        cost_estimate=attention_cost(1, 0),
        name="attend",
    )(info, vu, other, weights)


def back_v_kernel(
    info,
    vu_ref,
    att_ref,
    stats_ref,
    weight_hbm,
    out_ref,
    sib_ref,
    grad_t_ref,
    grad_ref,
    dv_ref,
    weight_ref,
    sems,
):
    length, core = info[0], info[1]
    arrive = fetch_tiles(length, weight_hbm, weight_ref, sems)
    width = HEADS * HEAD_DIM
    stat = [[stats_ref[head, s : s + 1, :] for s in range(4)] for head in range(HEADS)]
    mean = sum(row[0] for row in stat) * (1.0 / HEADS)
    square = sum(row[1] + HEAD_DIM * (row[0] - mean) * (row[0] - mean) for row in stat)
    inverse = lax.rsqrt(square * (1.0 / width) + EPSILON)
    up_mean = sum(row[2] for row in stat) * (1.0 / width)
    cross = sum(row[3] + (row[0] - mean) * row[2] for row in stat) * inverse * (1.0 / width)
    for m in range(CHIPS):
        where = rows_of(m)
        up = vu_ref[m, 1].astype(F32).T
        hat = (att_ref[:, where] - mean[:, where]) * inverse[:, where]
        out_ref[m, 1] = hat.T.astype(BF16)
        grad = inverse[:, where] * (up - up_mean[:, where] - hat * cross[:, where])
        grad_t_ref[:, where] = grad.astype(BF16)
        grad_ref[where, :] = grad.T.astype(BF16)

    def work(j):
        arrive(j)
        for m in range(j, CHIPS):
            term = dot(weight_ref[tile_of(j, m)], grad_ref[rows_of(m), :])
            if m == j:
                dv_ref[keys_of(j), :] = term
            else:
                dv_ref[keys_of(j), :] += term

    def dead(j):
        dv_ref[keys_of(j), :] = jnp.zeros((KEY_TILE, HEAD_DIM), F32)

    each_tile(length, work, dead)
    share(core, dv_ref, 1.0, out_ref, sib_ref)


def share(core, sum_ref, scale, out_ref, sib_ref):
    for chip in range(CHIPS):
        kept = pl.ds(pl.multiple_of((2 * chip + core) * ROWS, ROWS), ROWS)
        sent = pl.ds(pl.multiple_of((2 * chip + 1 - core) * ROWS, ROWS), ROWS)
        out_ref[chip, 0] = (sum_ref[kept, :] * scale).astype(BF16)
        sib_ref[chip] = (sum_ref[sent, :] * scale).astype(BF16)


def back_v(info, vu, att, stats, weights):
    half = CHIPS * ROWS
    return pl.pallas_call(
        back_v_kernel,
        out_shape=[
            jax.ShapeDtypeStruct((CHIPS, 2, ROWS, HEAD_DIM), BF16),
            jax.ShapeDtypeStruct((CHIPS, ROWS, HEAD_DIM), BF16),
            jax.ShapeDtypeStruct((HEAD_DIM, half), BF16),
        ],
        in_specs=[sspec(), vspec(), vspec(), vspec(), hspec()],
        out_specs=[vspec(), vspec(), vspec()],
        scratch_shapes=[
            VMEM((half, HEAD_DIM), BF16),
            VMEM((2 * half, HEAD_DIM), F32),
            VMEM((TILES, KEY_TILE, ROWS), BF16),
            pltpu.SemaphoreType.DMA((CHIPS,)),
        ],
        compiler_params=params(ATTN),
        cost_estimate=attention_cost(1, 0),
        name="back_v",
    )(info, vu, att, stats, weights)


def back_kq_kernel(
    info,
    kq_ref,
    vu_ref,
    other_ref,
    other_key_ref,
    slope_hbm,
    grad_t_ref,
    out_ref,
    sib_ref,
    value_ref,
    key_t_ref,
    dq_ref,
    dk_ref,
    slope_ref,
    sems,
):
    length, core = info[0], info[1]
    arrive = fetch_tiles(length, slope_hbm, slope_ref, sems)
    lay_rows(info, vu_ref, other_ref, value_ref)
    dq_ref[...] = jnp.zeros_like(dq_ref)
    for chip in range(CHIPS):
        for rows, side in ((kq_ref[chip, 0], core), (other_key_ref[chip], 1 - core)):
            start = pl.multiple_of((2 * chip + side) * ROWS, ROWS)
            key_t_ref[:, pl.ds(start, ROWS)] = rows.T

    def work(j):
        arrive(j)
        for m in range(j, CHIPS):
            grad = dot(value_ref[keys_of(j), :], grad_t_ref[:, rows_of(m)])
            slope = slope_ref[tile_of(j, m)].astype(F32)
            slope_ref[tile_of(j, m)] = (grad * slope).astype(BF16)
        for m in range(j, CHIPS):
            grad = slope_ref[tile_of(j, m)]
            dk = dot(grad, kq_ref[m, 1])
            dq = dot(key_t_ref[:, keys_of(j)], grad)
            if m == j:
                dk_ref[keys_of(j), :] = dk
            else:
                dk_ref[keys_of(j), :] += dk
            dq_ref[:, rows_of(m)] += dq

    def dead(j):
        dk_ref[keys_of(j), :] = jnp.zeros((KEY_TILE, HEAD_DIM), F32)

    each_tile(length, work, dead)
    for m in range(CHIPS):
        out_ref[m, 1] = (dq_ref[:, rows_of(m)].T * SCALE).astype(BF16)
    share(core, dk_ref, SCALE, out_ref, sib_ref)


def back_kq(info, kq, vu, other, other_keys, slope, grad_t):
    half = CHIPS * ROWS
    return pl.pallas_call(
        back_kq_kernel,
        out_shape=[
            jax.ShapeDtypeStruct((CHIPS, 2, ROWS, HEAD_DIM), BF16),
            jax.ShapeDtypeStruct((CHIPS, ROWS, HEAD_DIM), BF16),
        ],
        in_specs=[sspec()] + [vspec()] * 4 + [hspec(), vspec()],
        out_specs=[vspec(), vspec()],
        scratch_shapes=[
            VMEM((2 * half, HEAD_DIM), BF16),
            VMEM((HEAD_DIM, 2 * half), BF16),
            VMEM((HEAD_DIM, half), F32),
            VMEM((2 * half, HEAD_DIM), F32),
            VMEM((TILES, KEY_TILE, ROWS), BF16),
            pltpu.SemaphoreType.DMA((CHIPS,)),
        ],
        compiler_params=params(ATTN),
        cost_estimate=attention_cost(3, 0),
        name="back_kq",
    )(info, kq, vu, other, other_keys, slope, grad_t)


def merge_kernel(out_ref, sib_ref, *refs):
    done_ref = refs[-1]
    done_ref[:, 0] = (out_ref[:, 0].astype(F32) + sib_ref[...].astype(F32)).astype(BF16)
    done_ref[:, 1] = out_ref[:, 1]


def merge(out, sib, *kept):
    return pl.pallas_call(
        merge_kernel,
        out_shape=jax.ShapeDtypeStruct(out.shape, out.dtype),
        in_specs=[vspec(), vspec()] + [vspec() for _ in kept],
        out_specs=vspec(),
        compiler_params=params(SMALL),
        name="merge",
    )(out, sib, *kept)


def gather(back_ref, part, chunk):
    heads = CHUNK // HEAD_DIM
    blocks = [back_ref[chunk * heads + head, part].astype(F32) for head in range(heads)]
    return jnp.concatenate(blocks, axis=1)


def finish_vg_kernel(
    back_ref,
    gate_ref,
    slope_ref,
    hist_ref,
    up_ref,
    w_hbm,
    w_out_ref,
    mixed_ref,
    sum_ref,
    w_ref,
    sems,
):
    width = hist_ref.shape[1]
    arrive = start_weights(w_hbm, w_ref, sems, (1, 0))
    mixed = hist_ref[...].astype(F32)
    total = jnp.zeros(hist_ref.shape, F32)
    for part in range(2):
        for chunk, columns in chunks(width):
            grad = gather(back_ref, part, chunk)
            if part:
                gated = (grad * gate_ref[:, columns].astype(F32)).astype(BF16)
                mixed = mixed + dot(gated, w_out_ref[columns, :])
                grad = grad * up_ref[:, columns]
            pre = (grad * slope_ref[part, :, columns].astype(F32)).astype(BF16)
            arrive(part, chunk)
            total = total + dot_nt(pre, w_ref[part * (width // CHUNK) + chunk])
    mixed_ref[...] = mixed.astype(BF16)
    sum_ref[...] = total


def finish_vg(back, gate, slope, history, upstream, w_in, w_out):
    rows, width = history.shape
    return pl.pallas_call(
        finish_vg_kernel,
        in_specs=[vspec()] * 5 + [hspec(), vspec()],
        out_specs=[vspec(), vspec()],
        scratch_shapes=weight_scratch(width),
        out_shape=[
            jax.ShapeDtypeStruct((rows, width), BF16),
            jax.ShapeDtypeStruct((rows, width), F32),
        ],
        compiler_params=params(DENSE),
        name="finish_vg",
    )(back, gate, slope, history, upstream, w_in, w_out)


def finish_kq_kernel(
    back_in,
    slope_in,
    hist_in,
    start_in,
    cot_in,
    place_ref,
    w_hbm,
    rows_ref,
    w_ref,
    sems,
    back_ref,
    slope_ref,
    hist_ref,
    start_ref,
    cot_ref,
    in_sems,
):
    width = hist_ref.shape[1]
    pairs = [
        (hist_in, hist_ref),
        (back_in, back_ref),
        (slope_in, slope_ref),
        (start_in, start_ref),
        (cot_in, cot_ref),
    ]
    copies = [pltpu.make_async_copy(a, b, in_sems.at[i]) for i, (a, b) in enumerate(pairs)]
    for copy in copies[:3]:
        copy.start()
    arrive = start_weights(w_hbm, w_ref, sems, (3, 2))
    for copy in copies[3:]:
        copy.start()
    copies[0].wait()
    hat, inverse = normalize(hist_ref[...].astype(F32))
    copies[1].wait()
    copies[2].wait()
    grad = jnp.zeros(hist_ref.shape, F32)
    for part in range(2):
        for chunk, columns in chunks(width):
            pre = gather(back_ref, part, chunk) * slope_ref[part, :, columns].astype(F32)
            arrive(part, chunk)
            grad = grad + dot_nt(pre.astype(BF16), w_ref[part * (width // CHUNK) + chunk])
    copies[3].wait()
    grad = grad + start_ref[...]
    grad = inverse * (grad - row_mean(grad) - hat * row_mean(grad * hat))
    copies[4].wait()
    grad = (grad + cot_ref[...].astype(F32)).astype(BF16)
    rows_ref[...] = dot(onehot(place_ref[...]), grad).astype(BF16).reshape(rows_ref.shape)


def finish_kq(back, slope, history, start, cotangent, place, w_in):
    rows, width = history.shape
    return pl.pallas_call(
        finish_kq_kernel,
        in_specs=[hspec()] * 5 + [vspec(), hspec()],
        out_specs=vspec(),
        scratch_shapes=weight_scratch(width)
        + [
            VMEM((CHIPS, 2, ROWS, HEAD_DIM), BF16),
            VMEM((2, rows, width), BF16),
            VMEM((rows, width), BF16),
            VMEM((rows, width), F32),
            VMEM((rows, width), BF16),
            pltpu.SemaphoreType.DMA((5,)),
        ],
        out_shape=jax.ShapeDtypeStruct((rows // 2, 2, width), BF16),
        compiler_params=params(DENSE),
        name="finish_kq",
    )(back, slope, history, start, cotangent, place, w_in)


def body(log_rows, send_order, place, hist_len, w_in, w_out, cotangent):
    seq_size = lax.axis_size("seq")
    seq_index = lax.axis_index("seq")
    spot = seq_index % GROUP
    length = jnp.take(hist_len[0], seq_index // GROUP)
    info = jnp.stack([length, spot % 2]).astype(jnp.int32)
    same_core = [list(range(g + c, g + GROUP, 2)) for g in range(0, seq_size, GROUP) for c in (0, 1)]
    swap = [(i, i ^ 1) for i in range(seq_size)]

    def to_all(block):
        return lax.all_to_all(block, ("dp", "seq"), split_axis=0, concat_axis=0, tiled=True)

    def to_group(block, members):
        return lax.all_to_all(
            block, "seq", split_axis=0, concat_axis=0, tiled=True, axis_index_groups=members
        )

    upstream = jnp.dot(cotangent, w_out.T, preferred_element_type=F32)
    arrived = to_all(pick_rows(log_rows, send_order))
    history, normed, slope_kq, kq = project_kq(info, arrived, place, w_in, upstream)
    kq = to_group(kq, same_core)
    gate, slope_vg, vu, token = project_vu(normed, w_in, upstream)
    other_keys = lax.ppermute(first_part(kq, token), "seq", swap)
    weights, slopes, token = weigh(info, kq, other_keys, token)
    vu = to_group(vu, same_core)
    other_values = lax.ppermute(first_part(vu, token), "seq", swap)
    att, stats = attend(info, vu, other_values, weights)
    stats = to_group(stats, same_core)
    out, sib, grad_t = back_v(info, vu, att, stats, weights)
    back_vh = merge(out, lax.ppermute(sib, "seq", swap), grad_t)
    out, sib = back_kq(info, kq, vu, other_values, other_keys, slopes, grad_t)
    back_vh = to_group(back_vh, same_core)
    back_kq_rows = merge(out, lax.ppermute(sib, "seq", swap))
    mixed, start = finish_vg(back_vh, gate, slope_vg, history, upstream, w_in, w_out)
    back_kq_rows = to_group(back_kq_rows, same_core)
    grads = finish_kq(back_kq_rows, slope_kq, history, start, cotangent, place, w_in)
    log_grad = unpick_rows(to_all(grads), send_order, F32)
    return (mixed, log_grad)


def solution(mesh):
    rows = P(("dp", "seq"), None)
    return jax.shard_map(
        body,
        mesh=mesh,
        in_specs=(rows, rows, rows, P("dp", None), P(), P(), rows),
        out_specs=(rows, rows),
        check_vma=False,
    )
```

```python
import functools
import math

import jax
import jax.numpy as jnp
from jax import lax
from jax.experimental import pallas as pl
from jax.experimental.pallas import tpu as pltpu
from jax.sharding import PartitionSpec as P

HEADS = 8
GROUP = 16
EPSILON = 1e-05
CHIPS = 8
ROWS = 256
HEAD_DIM = 128
MIB = 1024 * 1024
DENSE = 56
SMALL = 48
ATTN = 48
BF16 = jnp.bfloat16
F32 = jnp.float32
VMEM = pltpu.VMEM
SMEM = pltpu.SMEM


def params(mib):
    return pltpu.CompilerParams(vmem_limit_bytes=mib * MIB)


def vspec():
    return pl.BlockSpec(memory_space=VMEM)


def aspec():
    return pl.BlockSpec(memory_space=pl.ANY)


def hspec():
    return pl.BlockSpec(memory_space=pltpu.HBM)


def sspec():
    return pl.BlockSpec(memory_space=SMEM)


def dot(a, b):
    return jnp.dot(a, b, preferred_element_type=F32)


def dot_nt(a, b):
    return lax.dot_general(a, b, (((1,), (1,)), ((), ())), preferred_element_type=F32)


def dot_tn(a, b):
    return lax.dot_general(a, b, (((0,), (0,)), ((), ())), preferred_element_type=F32)


def onehot(order):
    count = order.shape[1]
    spots = lax.broadcasted_iota(jnp.int32, (count, count), 0)
    return jnp.where(spots == order, 1.0, 0.0).astype(BF16)


def row_mean(x):
    return jnp.mean(x, axis=-1, keepdims=True)


def normalize(inputs):
    centred = inputs - row_mean(inputs)
    inverse = lax.rsqrt(row_mean(centred * centred) + EPSILON)
    return centred * inverse, inverse


def pick_kernel(rows_ref, order_ref, out_ref):
    rows = dot_tn(onehot(order_ref[...]), rows_ref[...]).astype(out_ref.dtype)
    out_ref[...] = rows.reshape(out_ref.shape)


def pick_rows(rows, order):
    return pl.pallas_call(
        pick_kernel,
        out_shape=jax.ShapeDtypeStruct((rows.shape[0] // 2, 2, rows.shape[1]), rows.dtype),
        in_specs=[vspec(), vspec()],
        out_specs=vspec(),
        compiler_params=params(DENSE),
        name="pick_rows",
    )(rows, order)


def unpick_kernel(rows_ref, order_ref, out_ref):
    out_ref[...] = dot(onehot(order_ref[...]), rows_ref[...].reshape(out_ref.shape)).astype(
        out_ref.dtype
    )


def unpick_rows(rows, order, dtype):
    return pl.pallas_call(
        unpick_kernel,
        out_shape=jax.ShapeDtypeStruct((2 * rows.shape[0], rows.shape[2]), dtype),
        in_specs=[vspec(), vspec()],
        out_specs=vspec(),
        compiler_params=params(SMALL),
        name="unpick_rows",
    )(rows, order)


CHUNK = 512


def start_weights(w_hbm, w_ref, sems, blocks):
    width = w_hbm.shape[0]
    per = width // CHUNK

    def copy(slot, chunk):
        return pltpu.make_async_copy(
            w_hbm.at[:, pl.ds(blocks[slot] * width + chunk * CHUNK, CHUNK)],
            w_ref.at[slot * per + chunk],
            sems.at[slot * per + chunk],
        )

    for slot in range(len(blocks)):
        for chunk in range(per):
            copy(slot, chunk).start()
    return lambda slot, chunk: copy(slot, chunk).wait()


def chunks(width):
    return [(c, slice(c * CHUNK, (c + 1) * CHUNK)) for c in range(width // CHUNK)]


def activate(preact):
    sigmoid = jnp.tanh(preact * 0.5) * 0.5 + 0.5
    act = preact * sigmoid
    return act.astype(BF16), (sigmoid + act - act * sigmoid).astype(BF16)


def lay(buf_ref, part, chunk, block):
    heads = CHUNK // HEAD_DIM
    for head in range(heads):
        buf_ref[chunk * heads + head, part] = block[:, head * HEAD_DIM : (head + 1) * HEAD_DIM]


def project_kq_kernel(
    info,
    arrived_ref,
    place_ref,
    w_hbm,
    _,
    hist_ref,
    normed_ref,
    slope_ref,
    buf_ref,
    w_ref,
    sems,
):
    rows, width = hist_ref.shape
    arrive = start_weights(w_hbm, w_ref, sems, (3, 2))
    history = dot_tn(onehot(place_ref[...]), arrived_ref[...].reshape(rows, width))
    hist_ref[...] = history.astype(BF16)
    normed = normalize(history)[0].astype(BF16)
    normed_ref[...] = normed
    for part in range(2):
        for chunk, columns in chunks(width):
            arrive(part, chunk)
            act, slope = activate(dot(normed, w_ref[part * (width // CHUNK) + chunk]))
            slope_ref[part, :, columns] = slope
            lay(buf_ref, part, chunk, act)


def project_vu_kernel(
    normed_ref, w_hbm, up_ref, gate_ref, slope_ref, buf_ref, token_ref, w_ref, sems
):
    width = normed_ref.shape[1]
    arrive = start_weights(w_hbm, w_ref, sems, (1, 0))
    normed = normed_ref[...]
    for part in range(2):
        for chunk, columns in chunks(width):
            arrive(part, chunk)
            act, slope = activate(dot(normed, w_ref[part * (width // CHUNK) + chunk]))
            slope_ref[part, :, columns] = slope
            if part:
                gate_ref[:, columns] = act
                act = (up_ref[:, columns] * act.astype(F32)).astype(BF16)
            lay(buf_ref, part, chunk, act)
    token_ref[...] = jnp.zeros_like(token_ref)


def weight_scratch(width):
    count = 2 * (width // CHUNK)
    return [VMEM((count, width, CHUNK), BF16), pltpu.SemaphoreType.DMA((count,))]


def project_kq(info, arrived, place, w_in, upstream):
    rows, width = upstream.shape
    return pl.pallas_call(
        project_kq_kernel,
        in_specs=[sspec(), vspec(), vspec(), hspec(), aspec()],
        out_specs=[vspec()] * 4,
        out_shape=[
            jax.ShapeDtypeStruct((rows, width), BF16),
            jax.ShapeDtypeStruct((rows, width), BF16),
            jax.ShapeDtypeStruct((2, rows, width), BF16),
            jax.ShapeDtypeStruct((CHIPS, 2, ROWS, HEAD_DIM), BF16),
        ],
        scratch_shapes=weight_scratch(width),
        compiler_params=params(DENSE),
        name="project_kq",
    )(info, arrived, place, w_in, upstream)


def project_vu(normed, w_in, upstream):
    rows, width = normed.shape
    return pl.pallas_call(
        project_vu_kernel,
        in_specs=[vspec(), hspec(), vspec()],
        out_specs=[vspec()] * 4,
        out_shape=[
            jax.ShapeDtypeStruct((rows, width), BF16),
            jax.ShapeDtypeStruct((2, rows, width), BF16),
            jax.ShapeDtypeStruct((CHIPS, 2, ROWS, HEAD_DIM), BF16),
            jax.ShapeDtypeStruct((8, HEAD_DIM), F32),
        ],
        scratch_shapes=weight_scratch(width),
        compiler_params=params(DENSE),
        name="project_vu",
    )(normed, w_in, upstream)


def part_kernel(pair_ref, _, out_ref):
    out_ref[...] = pair_ref[:, 0]


def first_part(pair, after):
    chips, _, rows, width = pair.shape
    return pl.pallas_call(
        part_kernel,
        out_shape=jax.ShapeDtypeStruct((chips, rows, width), pair.dtype),
        in_specs=[vspec(), aspec()],
        out_specs=vspec(),
        compiler_params=params(SMALL),
        name="first_part",
    )(pair, after)


TILES = CHIPS * (CHIPS + 1) // 2
KEY_TILE = 2 * ROWS
SCALE = 0.5 / math.sqrt(HEAD_DIM)


def tile_of(j, m):
    return j * CHIPS - j * (j - 1) // 2 + m - j


def lay_rows(info, own_ref, other_ref, out_ref):
    length, core = info[0], info[1]
    for chip in range(CHIPS):
        for source, side in ((own_ref.at[chip, 0], core), (other_ref.at[chip], 1 - core)):
            start = pl.multiple_of((2 * chip + side) * ROWS, ROWS)
            out_ref[pl.ds(start, ROWS), :] = source[...]

    @pl.when(length < GROUP * ROWS)
    def _():
        def clear(block, carry):
            where = pl.ds(pl.multiple_of(block * ROWS, ROWS), ROWS)
            spots = lax.broadcasted_iota(jnp.int32, (ROWS, HEAD_DIM), 0) + block * ROWS
            rows = jnp.where(spots < length, out_ref[where, :].astype(F32), 0.0)
            out_ref[where, :] = rows.astype(BF16)
            return carry

        lax.fori_loop(length // ROWS, GROUP, clear, 0)


def each_tile(length, work, dead=None, order=range(CHIPS)[::-1]):
    for j in order:
        if j == 0:
            work(0)
            continue
        pl.when(KEY_TILE * j < length)(functools.partial(work, j))
        if dead is not None:
            pl.when(KEY_TILE * j >= length)(functools.partial(dead, j))


def tiles_of(j):
    return pl.ds(tile_of(j, j), CHIPS - j)


def fetch_tiles(length, kept_ref, here_ref, sems):
    def copy(j):
        return pltpu.make_async_copy(kept_ref.at[tiles_of(j)], here_ref.at[tiles_of(j)], sems.at[j])

    each_tile(length, lambda j: copy(j).start())
    return lambda j: copy(j).wait()


def keys_of(j):
    return slice(KEY_TILE * j, KEY_TILE * (j + 1))


def rows_of(m):
    return slice(ROWS * m, ROWS * (m + 1))


def weigh_kernel(
    info,
    kq_ref,
    other_ref,
    _,
    weight_out,
    slope_out,
    token_ref,
    key_ref,
    query_t_ref,
    weight_ref,
    slope_ref,
    weight_sems,
    slope_sems,
):
    length, core = info[0], info[1]

    def copies(j):
        where = tiles_of(j)
        return (
            pltpu.make_async_copy(weight_ref.at[where], weight_out.at[where], weight_sems.at[j]),
            pltpu.make_async_copy(slope_ref.at[where], slope_out.at[where], slope_sems.at[j]),
        )

    lay_rows(info, kq_ref, other_ref, key_ref)
    for m in range(CHIPS):
        query_t_ref[:, rows_of(m)] = (kq_ref[m, 1].astype(F32) * SCALE).astype(BF16).T

    def work(j):
        for m in range(j, CHIPS):
            half = dot(key_ref[keys_of(j), :], query_t_ref[:, rows_of(m)])
            tanh = jnp.tanh(half)
            weights = half * (1.0 + tanh)
            slope = (1.0 + tanh) + weights * (1.0 - tanh)
            if m == j:
                query_spot = lax.broadcasted_iota(jnp.int32, (KEY_TILE, ROWS), 1) + core * ROWS
                key_spot = lax.broadcasted_iota(jnp.int32, (KEY_TILE, ROWS), 0)
                allowed = key_spot <= query_spot
                weights = jnp.where(allowed, weights, 0.0)
                slope = jnp.where(allowed, slope, 0.0)
            weight_ref[tile_of(j, m)] = weights.astype(BF16)
            slope_ref[tile_of(j, m)] = slope.astype(BF16)
        for copy in copies(j):
            copy.start()

    def drain(j):
        for copy in copies(j):
            copy.wait()

    each_tile(length, work, order=range(CHIPS))
    token_ref[...] = jnp.zeros_like(token_ref)
    each_tile(length, drain)


def attention_cost(matmuls, exps):
    area = TILES * KEY_TILE * ROWS
    return pl.CostEstimate(
        flops=4 * matmuls * area * HEAD_DIM, bytes_accessed=4 * area, transcendentals=exps * area
    )


def weigh(info, kq, other, after):
    half = CHIPS * ROWS
    return pl.pallas_call(
        weigh_kernel,
        out_shape=[
            jax.ShapeDtypeStruct((TILES, KEY_TILE, ROWS), BF16),
            jax.ShapeDtypeStruct((TILES, KEY_TILE, ROWS), BF16),
            jax.ShapeDtypeStruct((8, HEAD_DIM), F32),
        ],
        in_specs=[sspec(), vspec(), vspec(), aspec()],
        out_specs=[hspec(), hspec(), vspec()],
        scratch_shapes=[
            VMEM((2 * half, HEAD_DIM), BF16),
            VMEM((HEAD_DIM, half), BF16),
            VMEM((TILES, KEY_TILE, ROWS), BF16),
            VMEM((TILES, KEY_TILE, ROWS), BF16),
            pltpu.SemaphoreType.DMA((CHIPS,)),
            pltpu.SemaphoreType.DMA((CHIPS,)),
        ],
        compiler_params=params(ATTN),
        cost_estimate=attention_cost(1, 1),
        name="weigh",
    )(info, kq, other, after)


def attend_kernel(
    info,
    vu_ref,
    other_ref,
    weight_hbm,
    att_ref,
    stats_ref,
    value_ref,
    value_t_ref,
    weight_ref,
    sems,
):
    length = info[0]
    arrive = fetch_tiles(length, weight_hbm, weight_ref, sems)
    lay_rows(info, vu_ref, other_ref, value_ref)
    att_ref[...] = jnp.zeros_like(att_ref)

    def work(j):
        arrive(j)
        for block in (2 * j, 2 * j + 1):
            value_t_ref[:, rows_of(block)] = value_ref[rows_of(block), :].T
        for m in range(j, CHIPS):
            att_ref[:, rows_of(m)] += dot(value_t_ref[:, keys_of(j)], weight_ref[tile_of(j, m)])

    each_tile(length, work)
    for m in range(CHIPS):
        att = att_ref[:, rows_of(m)]
        up = vu_ref[m, 1].T.astype(F32)
        mean = jnp.mean(att, axis=0, keepdims=True)
        centred = att - mean
        stats = jnp.concatenate(
            [
                mean,
                jnp.sum(centred * centred, axis=0, keepdims=True),
                jnp.sum(up, axis=0, keepdims=True),
                jnp.sum(up * centred, axis=0, keepdims=True),
            ],
            axis=0,
        )
        for head in range(HEADS):
            stats_ref[head, :, rows_of(m)] = stats


def attend(info, vu, other, weights):
    half = CHIPS * ROWS
    return pl.pallas_call(
        attend_kernel,
        out_shape=[
            jax.ShapeDtypeStruct((HEAD_DIM, half), F32),
            jax.ShapeDtypeStruct((HEADS, 4, half), F32),
        ],
        in_specs=[sspec(), vspec(), vspec(), hspec()],
        out_specs=[vspec(), vspec()],
        scratch_shapes=[
            VMEM((2 * half, HEAD_DIM), BF16),
            VMEM((HEAD_DIM, 2 * half), BF16),
            VMEM((TILES, KEY_TILE, ROWS), BF16),
            pltpu.SemaphoreType.DMA((CHIPS,)),
        ],
        compiler_params=params(ATTN),
        cost_estimate=attention_cost(1, 0),
        name="attend",
    )(info, vu, other, weights)


def back_v_kernel(
    info,
    vu_ref,
    att_ref,
    stats_ref,
    weight_hbm,
    out_ref,
    sib_ref,
    grad_t_ref,
    grad_ref,
    dv_ref,
    weight_ref,
    sems,
):
    length, core = info[0], info[1]
    arrive = fetch_tiles(length, weight_hbm, weight_ref, sems)
    width = HEADS * HEAD_DIM
    stat = [[stats_ref[head, s : s + 1, :] for s in range(4)] for head in range(HEADS)]
    mean = sum(row[0] for row in stat) * (1.0 / HEADS)
    square = sum(row[1] + HEAD_DIM * (row[0] - mean) * (row[0] - mean) for row in stat)
    inverse = lax.rsqrt(square * (1.0 / width) + EPSILON)
    up_mean = sum(row[2] for row in stat) * (1.0 / width)
    cross = sum(row[3] + (row[0] - mean) * row[2] for row in stat) * inverse * (1.0 / width)
    for m in range(CHIPS):
        where = rows_of(m)
        up = vu_ref[m, 1].T.astype(F32)
        hat = (att_ref[:, where] - mean[:, where]) * inverse[:, where]
        out_ref[m, 1] = hat.astype(BF16).T
        grad = inverse[:, where] * (up - up_mean[:, where] - hat * cross[:, where])
        grad = grad.astype(BF16)
        grad_t_ref[:, where] = grad
        grad_ref[where, :] = grad.T

    def work(j):
        arrive(j)
        for m in range(j, CHIPS):
            term = dot(weight_ref[tile_of(j, m)], grad_ref[rows_of(m), :])
            if m == j:
                dv_ref[keys_of(j), :] = term
            else:
                dv_ref[keys_of(j), :] += term

    def dead(j):
        dv_ref[keys_of(j), :] = jnp.zeros((KEY_TILE, HEAD_DIM), F32)

    each_tile(length, work, dead)
    share(core, dv_ref, 1.0, out_ref, sib_ref)


def share(core, sum_ref, scale, out_ref, sib_ref):
    for chip in range(CHIPS):
        kept = pl.ds(pl.multiple_of((2 * chip + core) * ROWS, ROWS), ROWS)
        sent = pl.ds(pl.multiple_of((2 * chip + 1 - core) * ROWS, ROWS), ROWS)
        out_ref[chip, 0] = (sum_ref[kept, :] * scale).astype(BF16)
        sib_ref[chip] = (sum_ref[sent, :] * scale).astype(BF16)


def back_v(info, vu, att, stats, weights):
    half = CHIPS * ROWS
    return pl.pallas_call(
        back_v_kernel,
        out_shape=[
            jax.ShapeDtypeStruct((CHIPS, 2, ROWS, HEAD_DIM), BF16),
            jax.ShapeDtypeStruct((CHIPS, ROWS, HEAD_DIM), BF16),
            jax.ShapeDtypeStruct((HEAD_DIM, half), BF16),
        ],
        in_specs=[sspec(), vspec(), vspec(), vspec(), hspec()],
        out_specs=[vspec(), vspec(), vspec()],
        scratch_shapes=[
            VMEM((half, HEAD_DIM), BF16),
            VMEM((2 * half, HEAD_DIM), F32),
            VMEM((TILES, KEY_TILE, ROWS), BF16),
            pltpu.SemaphoreType.DMA((CHIPS,)),
        ],
        compiler_params=params(ATTN),
        cost_estimate=attention_cost(1, 0),
        name="back_v",
    )(info, vu, att, stats, weights)


def back_kq_kernel(
    info,
    kq_ref,
    vu_ref,
    other_ref,
    other_key_ref,
    slope_hbm,
    grad_t_ref,
    out_ref,
    sib_ref,
    value_ref,
    key_t_ref,
    dq_ref,
    dk_ref,
    slope_ref,
    sems,
):
    length, core = info[0], info[1]
    arrive = fetch_tiles(length, slope_hbm, slope_ref, sems)
    lay_rows(info, vu_ref, other_ref, value_ref)
    dq_ref[...] = jnp.zeros_like(dq_ref)
    for chip in range(CHIPS):
        for rows, side in ((kq_ref[chip, 0], core), (other_key_ref[chip], 1 - core)):
            start = pl.multiple_of((2 * chip + side) * ROWS, ROWS)
            key_t_ref[:, pl.ds(start, ROWS)] = rows.T

    def work(j):
        arrive(j)
        for m in range(j, CHIPS):
            grad = dot(value_ref[keys_of(j), :], grad_t_ref[:, rows_of(m)])
            slope = slope_ref[tile_of(j, m)].astype(F32)
            slope_ref[tile_of(j, m)] = (grad * slope).astype(BF16)
        for m in range(j, CHIPS):
            grad = slope_ref[tile_of(j, m)]
            dk = dot(grad, kq_ref[m, 1])
            dq = dot(key_t_ref[:, keys_of(j)], grad)
            if m == j:
                dk_ref[keys_of(j), :] = dk
            else:
                dk_ref[keys_of(j), :] += dk
            dq_ref[:, rows_of(m)] += dq

    def dead(j):
        dk_ref[keys_of(j), :] = jnp.zeros((KEY_TILE, HEAD_DIM), F32)

    each_tile(length, work, dead)
    for m in range(CHIPS):
        out_ref[m, 1] = (dq_ref[:, rows_of(m)] * SCALE).astype(BF16).T
    share(core, dk_ref, SCALE, out_ref, sib_ref)


def back_kq(info, kq, vu, other, other_keys, slope, grad_t):
    half = CHIPS * ROWS
    return pl.pallas_call(
        back_kq_kernel,
        out_shape=[
            jax.ShapeDtypeStruct((CHIPS, 2, ROWS, HEAD_DIM), BF16),
            jax.ShapeDtypeStruct((CHIPS, ROWS, HEAD_DIM), BF16),
        ],
        in_specs=[sspec()] + [vspec()] * 4 + [hspec(), vspec()],
        out_specs=[vspec(), vspec()],
        scratch_shapes=[
            VMEM((2 * half, HEAD_DIM), BF16),
            VMEM((HEAD_DIM, 2 * half), BF16),
            VMEM((HEAD_DIM, half), F32),
            VMEM((2 * half, HEAD_DIM), F32),
            VMEM((TILES, KEY_TILE, ROWS), BF16),
            pltpu.SemaphoreType.DMA((CHIPS,)),
        ],
        compiler_params=params(ATTN),
        cost_estimate=attention_cost(3, 0),
        name="back_kq",
    )(info, kq, vu, other, other_keys, slope, grad_t)


def merge_kernel(out_ref, sib_ref, *refs):
    done_ref = refs[-1]
    done_ref[:, 0] = (out_ref[:, 0].astype(F32) + sib_ref[...].astype(F32)).astype(BF16)
    done_ref[:, 1] = out_ref[:, 1]


def merge(out, sib, *kept):
    return pl.pallas_call(
        merge_kernel,
        out_shape=jax.ShapeDtypeStruct(out.shape, out.dtype),
        in_specs=[vspec(), vspec()] + [vspec() for _ in kept],
        out_specs=vspec(),
        compiler_params=params(SMALL),
        name="merge",
    )(out, sib, *kept)


def gather(back_ref, part, chunk):
    heads = CHUNK // HEAD_DIM
    blocks = [back_ref[chunk * heads + head, part].astype(F32) for head in range(heads)]
    return jnp.concatenate(blocks, axis=1)


def finish_vg_kernel(
    back_ref,
    gate_ref,
    slope_ref,
    hist_ref,
    up_ref,
    w_hbm,
    w_out_ref,
    mixed_ref,
    sum_ref,
    w_ref,
    sems,
):
    width = hist_ref.shape[1]
    arrive = start_weights(w_hbm, w_ref, sems, (1, 0))
    mixed = hist_ref[...].astype(F32)
    total = jnp.zeros(hist_ref.shape, F32)
    for part in range(2):
        for chunk, columns in chunks(width):
            grad = gather(back_ref, part, chunk)
            if part:
                gated = (grad * gate_ref[:, columns].astype(F32)).astype(BF16)
                mixed = mixed + dot(gated, w_out_ref[columns, :])
                grad = grad * up_ref[:, columns]
            pre = (grad * slope_ref[part, :, columns].astype(F32)).astype(BF16)
            arrive(part, chunk)
            total = total + dot_nt(pre, w_ref[part * (width // CHUNK) + chunk])
    mixed_ref[...] = mixed.astype(BF16)
    sum_ref[...] = total


def finish_vg(back, gate, slope, history, upstream, w_in, w_out):
    rows, width = history.shape
    return pl.pallas_call(
        finish_vg_kernel,
        in_specs=[vspec()] * 5 + [hspec(), vspec()],
        out_specs=[vspec(), vspec()],
        scratch_shapes=weight_scratch(width),
        out_shape=[
            jax.ShapeDtypeStruct((rows, width), BF16),
            jax.ShapeDtypeStruct((rows, width), F32),
        ],
        compiler_params=params(DENSE),
        name="finish_vg",
    )(back, gate, slope, history, upstream, w_in, w_out)


def finish_kq_kernel(
    back_in,
    slope_in,
    hist_in,
    start_in,
    cot_in,
    place_ref,
    w_hbm,
    rows_ref,
    w_ref,
    sems,
    back_ref,
    slope_ref,
    hist_ref,
    start_ref,
    cot_ref,
    in_sems,
):
    width = hist_ref.shape[1]
    pairs = [
        (hist_in, hist_ref),
        (back_in, back_ref),
        (slope_in, slope_ref),
        (start_in, start_ref),
        (cot_in, cot_ref),
    ]
    copies = [pltpu.make_async_copy(a, b, in_sems.at[i]) for i, (a, b) in enumerate(pairs)]
    for copy in copies[:3]:
        copy.start()
    arrive = start_weights(w_hbm, w_ref, sems, (3, 2))
    for copy in copies[3:]:
        copy.start()
    copies[0].wait()
    hat, inverse = normalize(hist_ref[...].astype(F32))
    copies[1].wait()
    copies[2].wait()
    grad = jnp.zeros(hist_ref.shape, F32)
    for part in range(2):
        for chunk, columns in chunks(width):
            pre = gather(back_ref, part, chunk) * slope_ref[part, :, columns].astype(F32)
            arrive(part, chunk)
            grad = grad + dot_nt(pre.astype(BF16), w_ref[part * (width // CHUNK) + chunk])
    copies[3].wait()
    grad = grad + start_ref[...]
    grad = inverse * (grad - row_mean(grad) - hat * row_mean(grad * hat))
    copies[4].wait()
    grad = (grad + cot_ref[...].astype(F32)).astype(BF16)
    rows_ref[...] = dot(onehot(place_ref[...]), grad).astype(BF16).reshape(rows_ref.shape)


def finish_kq(back, slope, history, start, cotangent, place, w_in):
    rows, width = history.shape
    return pl.pallas_call(
        finish_kq_kernel,
        in_specs=[hspec()] * 5 + [vspec(), hspec()],
        out_specs=vspec(),
        scratch_shapes=weight_scratch(width)
        + [
            VMEM((CHIPS, 2, ROWS, HEAD_DIM), BF16),
            VMEM((2, rows, width), BF16),
            VMEM((rows, width), BF16),
            VMEM((rows, width), F32),
            VMEM((rows, width), BF16),
            pltpu.SemaphoreType.DMA((5,)),
        ],
        out_shape=jax.ShapeDtypeStruct((rows // 2, 2, width), BF16),
        compiler_params=params(DENSE),
        name="finish_kq",
    )(back, slope, history, start, cotangent, place, w_in)


def body(log_rows, send_order, place, hist_len, w_in, w_out, cotangent):
    seq_size = lax.axis_size("seq")
    seq_index = lax.axis_index("seq")
    spot = seq_index % GROUP
    length = jnp.take(hist_len[0], seq_index // GROUP)
    info = jnp.stack([length, spot % 2]).astype(jnp.int32)
    same_core = [list(range(g + c, g + GROUP, 2)) for g in range(0, seq_size, GROUP) for c in (0, 1)]
    swap = [(i, i ^ 1) for i in range(seq_size)]

    def to_all(block):
        return lax.all_to_all(block, ("dp", "seq"), split_axis=0, concat_axis=0, tiled=True)

    def to_group(block, members):
        return lax.all_to_all(
            block, "seq", split_axis=0, concat_axis=0, tiled=True, axis_index_groups=members
        )

    upstream = jnp.dot(cotangent, w_out.T, preferred_element_type=F32)
    arrived = to_all(pick_rows(log_rows, send_order))
    history, normed, slope_kq, kq = project_kq(info, arrived, place, w_in, upstream)
    kq = to_group(kq, same_core)
    gate, slope_vg, vu, token = project_vu(normed, w_in, upstream)
    other_keys = lax.ppermute(first_part(kq, token), "seq", swap)
    weights, slopes, token = weigh(info, kq, other_keys, token)
    vu = to_group(vu, same_core)
    other_values = lax.ppermute(first_part(vu, token), "seq", swap)
    att, stats = attend(info, vu, other_values, weights)
    stats = to_group(stats, same_core)
    out, sib, grad_t = back_v(info, vu, att, stats, weights)
    back_vh = merge(out, lax.ppermute(sib, "seq", swap), grad_t)
    out, sib = back_kq(info, kq, vu, other_values, other_keys, slopes, grad_t)
    back_vh = to_group(back_vh, same_core)
    back_kq_rows = merge(out, lax.ppermute(sib, "seq", swap))
    mixed, start = finish_vg(back_vh, gate, slope_vg, history, upstream, w_in, w_out)
    back_kq_rows = to_group(back_kq_rows, same_core)
    grads = finish_kq(back_kq_rows, slope_kq, history, start, cotangent, place, w_in)
    log_grad = unpick_rows(to_all(grads), send_order, F32)
    return (mixed, log_grad)


def solution(mesh):
    rows = P(("dp", "seq"), None)
    return jax.shard_map(
        body,
        mesh=mesh,
        in_specs=(rows, rows, rows, P("dp", None), P(), P(), rows),
        out_specs=(rows, rows),
        check_vma=False,
    )
```

```python
import functools
import math

import jax
import jax.numpy as jnp
from jax import lax
from jax.experimental import pallas as pl
from jax.experimental.pallas import tpu as pltpu
from jax.sharding import PartitionSpec as P

HEADS = 8
GROUP = 16
EPSILON = 1e-05
CHIPS = 8
ROWS = 256
HEAD_DIM = 128
MIB = 1024 * 1024
DENSE = 56
SMALL = 48
ATTN = 48
BF16 = jnp.bfloat16
F32 = jnp.float32
VMEM = pltpu.VMEM
SMEM = pltpu.SMEM


def params(mib):
    return pltpu.CompilerParams(vmem_limit_bytes=mib * MIB)


def vspec():
    return pl.BlockSpec(memory_space=VMEM)


def aspec():
    return pl.BlockSpec(memory_space=pl.ANY)


def hspec():
    return pl.BlockSpec(memory_space=pltpu.HBM)


def sspec():
    return pl.BlockSpec(memory_space=SMEM)


def dot(a, b):
    return jnp.dot(a, b, preferred_element_type=F32)


def dot_nt(a, b):
    return lax.dot_general(a, b, (((1,), (1,)), ((), ())), preferred_element_type=F32)


def dot_tn(a, b):
    return lax.dot_general(a, b, (((0,), (0,)), ((), ())), preferred_element_type=F32)


def onehot(order):
    count = order.shape[1]
    spots = lax.broadcasted_iota(jnp.int32, (count, count), 0)
    return jnp.where(spots == order, 1.0, 0.0).astype(BF16)


def row_mean(x):
    return jnp.mean(x, axis=-1, keepdims=True)


def normalize(inputs):
    centred = inputs - row_mean(inputs)
    inverse = lax.rsqrt(row_mean(centred * centred) + EPSILON)
    return centred * inverse, inverse


def pick_kernel(rows_ref, order_ref, out_ref):
    rows = dot_tn(onehot(order_ref[...]), rows_ref[...]).astype(out_ref.dtype)
    out_ref[...] = rows.reshape(out_ref.shape)


def pick_rows(rows, order):
    return pl.pallas_call(
        pick_kernel,
        out_shape=jax.ShapeDtypeStruct((rows.shape[0] // 2, 2, rows.shape[1]), rows.dtype),
        in_specs=[vspec(), vspec()],
        out_specs=vspec(),
        compiler_params=params(DENSE),
        name="pick_rows",
    )(rows, order)


def unpick_kernel(rows_ref, order_ref, out_ref):
    out_ref[...] = dot(onehot(order_ref[...]), rows_ref[...].reshape(out_ref.shape)).astype(
        out_ref.dtype
    )


def unpick_rows(rows, order, dtype):
    return pl.pallas_call(
        unpick_kernel,
        out_shape=jax.ShapeDtypeStruct((2 * rows.shape[0], rows.shape[2]), dtype),
        in_specs=[vspec(), vspec()],
        out_specs=vspec(),
        compiler_params=params(SMALL),
        name="unpick_rows",
    )(rows, order)


CHUNK = 512


def start_weights(w_hbm, w_ref, sems, blocks):
    width = w_hbm.shape[0]
    per = width // CHUNK

    def copy(slot, chunk):
        return pltpu.make_async_copy(
            w_hbm.at[:, pl.ds(blocks[slot] * width + chunk * CHUNK, CHUNK)],
            w_ref.at[slot * per + chunk],
            sems.at[slot * per + chunk],
        )

    for slot in range(len(blocks)):
        for chunk in range(per):
            copy(slot, chunk).start()
    return lambda slot, chunk: copy(slot, chunk).wait()


def chunks(width):
    return [(c, slice(c * CHUNK, (c + 1) * CHUNK)) for c in range(width // CHUNK)]


def activate(preact):
    sigmoid = jnp.tanh(preact * 0.5) * 0.5 + 0.5
    act = preact * sigmoid
    return act.astype(BF16), (sigmoid + act - act * sigmoid).astype(BF16)


def lay(buf_ref, part, chunk, block):
    heads = CHUNK // HEAD_DIM
    for head in range(heads):
        buf_ref[chunk * heads + head, part] = block[:, head * HEAD_DIM : (head + 1) * HEAD_DIM]


def project_kq_kernel(
    info,
    arrived_ref,
    place_ref,
    w_hbm,
    _,
    hist_ref,
    normed_ref,
    slope_ref,
    buf_ref,
    w_ref,
    sems,
):
    rows, width = hist_ref.shape
    arrive = start_weights(w_hbm, w_ref, sems, (3, 2))
    history = dot_tn(onehot(place_ref[...]), arrived_ref[...].reshape(rows, width))
    hist_ref[...] = history.astype(BF16)
    normed = normalize(history)[0].astype(BF16)
    normed_ref[...] = normed
    for part in range(2):
        for chunk, columns in chunks(width):
            arrive(part, chunk)
            act, slope = activate(dot(normed, w_ref[part * (width // CHUNK) + chunk]))
            slope_ref[part, :, columns] = slope
            lay(buf_ref, part, chunk, act)


def project_vu_kernel(
    normed_ref, w_hbm, up_ref, gate_ref, slope_ref, buf_ref, token_ref, w_ref, sems
):
    width = normed_ref.shape[1]
    arrive = start_weights(w_hbm, w_ref, sems, (1, 0))
    normed = normed_ref[...]
    for part in range(2):
        for chunk, columns in chunks(width):
            arrive(part, chunk)
            act, slope = activate(dot(normed, w_ref[part * (width // CHUNK) + chunk]))
            slope_ref[part, :, columns] = slope
            if part:
                gate_ref[:, columns] = act
                act = (up_ref[:, columns] * act.astype(F32)).astype(BF16)
            lay(buf_ref, part, chunk, act)
    token_ref[...] = jnp.zeros_like(token_ref)


def weight_scratch(width):
    count = 2 * (width // CHUNK)
    return [VMEM((count, width, CHUNK), BF16), pltpu.SemaphoreType.DMA((count,))]


def project_kq(info, arrived, place, w_in, upstream):
    rows, width = upstream.shape
    return pl.pallas_call(
        project_kq_kernel,
        in_specs=[sspec(), vspec(), vspec(), hspec(), aspec()],
        out_specs=[vspec()] * 4,
        out_shape=[
            jax.ShapeDtypeStruct((rows, width), BF16),
            jax.ShapeDtypeStruct((rows, width), BF16),
            jax.ShapeDtypeStruct((2, rows, width), BF16),
            jax.ShapeDtypeStruct((CHIPS, 2, ROWS, HEAD_DIM), BF16),
        ],
        scratch_shapes=weight_scratch(width),
        compiler_params=params(DENSE),
        name="project_kq",
    )(info, arrived, place, w_in, upstream)


def project_vu(normed, w_in, upstream):
    rows, width = normed.shape
    return pl.pallas_call(
        project_vu_kernel,
        in_specs=[vspec(), hspec(), vspec()],
        out_specs=[vspec()] * 4,
        out_shape=[
            jax.ShapeDtypeStruct((rows, width), BF16),
            jax.ShapeDtypeStruct((2, rows, width), BF16),
            jax.ShapeDtypeStruct((CHIPS, 2, ROWS, HEAD_DIM), BF16),
            jax.ShapeDtypeStruct((8, HEAD_DIM), F32),
        ],
        scratch_shapes=weight_scratch(width),
        compiler_params=params(DENSE),
        name="project_vu",
    )(normed, w_in, upstream)


def part_kernel(pair_ref, _, out_ref):
    out_ref[...] = pair_ref[:, 0]


def first_part(pair, after):
    chips, _, rows, width = pair.shape
    return pl.pallas_call(
        part_kernel,
        out_shape=jax.ShapeDtypeStruct((chips, rows, width), pair.dtype),
        in_specs=[vspec(), aspec()],
        out_specs=vspec(),
        compiler_params=params(SMALL),
        name="first_part",
    )(pair, after)


TILES = CHIPS * (CHIPS + 1) // 2
KEY_TILE = 2 * ROWS
SCALE = 0.5 / math.sqrt(HEAD_DIM)


def tile_of(j, m):
    return j * CHIPS - j * (j - 1) // 2 + m - j


def lay_rows(info, own_ref, other_ref, out_ref):
    length, core = info[0], info[1]
    for chip in range(CHIPS):
        for source, side in ((own_ref.at[chip, 0], core), (other_ref.at[chip], 1 - core)):
            start = pl.multiple_of((2 * chip + side) * ROWS, ROWS)
            out_ref[pl.ds(start, ROWS), :] = source[...]

    @pl.when(length < GROUP * ROWS)
    def _():
        def clear(block, carry):
            where = pl.ds(pl.multiple_of(block * ROWS, ROWS), ROWS)
            spots = lax.broadcasted_iota(jnp.int32, (ROWS, HEAD_DIM), 0) + block * ROWS
            rows = jnp.where(spots < length, out_ref[where, :].astype(F32), 0.0)
            out_ref[where, :] = rows.astype(BF16)
            return carry

        lax.fori_loop(length // ROWS, GROUP, clear, 0)


def each_tile(length, work, dead=None, order=range(CHIPS)[::-1]):
    for j in order:
        if j == 0:
            work(0)
            continue
        pl.when(KEY_TILE * j < length)(functools.partial(work, j))
        if dead is not None:
            pl.when(KEY_TILE * j >= length)(functools.partial(dead, j))


def tiles_of(j):
    return pl.ds(tile_of(j, j), CHIPS - j)


def fetch_tiles(length, kept_ref, here_ref, sems):
    def copy(j):
        return pltpu.make_async_copy(kept_ref.at[tiles_of(j)], here_ref.at[tiles_of(j)], sems.at[j])

    each_tile(length, lambda j: copy(j).start())
    return lambda j: copy(j).wait()


def keys_of(j):
    return slice(KEY_TILE * j, KEY_TILE * (j + 1))


def rows_of(m):
    return slice(ROWS * m, ROWS * (m + 1))


def weigh_kernel(
    info,
    kq_ref,
    other_ref,
    _,
    weight_out,
    slope_out,
    token_ref,
    key_ref,
    query_t_ref,
    weight_ref,
    slope_ref,
    weight_sems,
    slope_sems,
):
    length, core = info[0], info[1]

    def copies(j):
        where = tiles_of(j)
        return (
            pltpu.make_async_copy(weight_ref.at[where], weight_out.at[where], weight_sems.at[j]),
            pltpu.make_async_copy(slope_ref.at[where], slope_out.at[where], slope_sems.at[j]),
        )

    lay_rows(info, kq_ref, other_ref, key_ref)
    for m in range(CHIPS):
        query_t_ref[:, rows_of(m)] = (kq_ref[m, 1].astype(F32) * SCALE).astype(BF16).T

    def work(j):
        for m in range(j, CHIPS):
            half = dot(key_ref[keys_of(j), :], query_t_ref[:, rows_of(m)])
            tanh = jnp.tanh(half)
            weights = half * (1.0 + tanh)
            slope = (1.0 + tanh) + weights * (1.0 - tanh)
            if m == j:
                query_spot = lax.broadcasted_iota(jnp.int32, (KEY_TILE, ROWS), 1) + core * ROWS
                key_spot = lax.broadcasted_iota(jnp.int32, (KEY_TILE, ROWS), 0)
                allowed = key_spot <= query_spot
                weights = jnp.where(allowed, weights, 0.0)
                slope = jnp.where(allowed, slope, 0.0)
            weight_ref[tile_of(j, m)] = weights.astype(BF16)
            slope_ref[tile_of(j, m)] = slope.astype(BF16)
        for copy in copies(j):
            copy.start()

    def drain(j):
        for copy in copies(j):
            copy.wait()

    each_tile(length, work, order=range(CHIPS))
    token_ref[...] = jnp.zeros_like(token_ref)
    each_tile(length, drain)


def attention_cost(matmuls, exps):
    area = TILES * KEY_TILE * ROWS
    return pl.CostEstimate(
        flops=4 * matmuls * area * HEAD_DIM, bytes_accessed=4 * area, transcendentals=exps * area
    )


def weigh(info, kq, other, after):
    half = CHIPS * ROWS
    return pl.pallas_call(
        weigh_kernel,
        out_shape=[
            jax.ShapeDtypeStruct((TILES, KEY_TILE, ROWS), BF16),
            jax.ShapeDtypeStruct((TILES, KEY_TILE, ROWS), BF16),
            jax.ShapeDtypeStruct((8, HEAD_DIM), F32),
        ],
        in_specs=[sspec(), vspec(), vspec(), aspec()],
        out_specs=[hspec(), hspec(), vspec()],
        scratch_shapes=[
            VMEM((2 * half, HEAD_DIM), BF16),
            VMEM((HEAD_DIM, half), BF16),
            VMEM((TILES, KEY_TILE, ROWS), BF16),
            VMEM((TILES, KEY_TILE, ROWS), BF16),
            pltpu.SemaphoreType.DMA((CHIPS,)),
            pltpu.SemaphoreType.DMA((CHIPS,)),
        ],
        compiler_params=params(ATTN),
        cost_estimate=attention_cost(1, 1),
        name="weigh",
    )(info, kq, other, after)


def attend_kernel(
    info,
    vu_ref,
    other_ref,
    weight_hbm,
    att_ref,
    stats_ref,
    value_ref,
    value_t_ref,
    weight_ref,
    sems,
):
    length = info[0]
    arrive = fetch_tiles(length, weight_hbm, weight_ref, sems)
    lay_rows(info, vu_ref, other_ref, value_ref)
    att_ref[...] = jnp.zeros_like(att_ref)

    def work(j):
        arrive(j)
        for block in (2 * j, 2 * j + 1):
            value_t_ref[:, rows_of(block)] = value_ref[rows_of(block), :].T
        for m in range(j, CHIPS):
            att_ref[:, rows_of(m)] += dot(value_t_ref[:, keys_of(j)], weight_ref[tile_of(j, m)])

    each_tile(length, work)
    for m in range(CHIPS):
        att = att_ref[:, rows_of(m)]
        up = vu_ref[m, 1].T.astype(F32)
        mean = jnp.mean(att, axis=0, keepdims=True)
        centred = att - mean
        stats = jnp.concatenate(
            [
                mean,
                jnp.sum(centred * centred, axis=0, keepdims=True),
                jnp.sum(up, axis=0, keepdims=True),
                jnp.sum(up * centred, axis=0, keepdims=True),
            ],
            axis=0,
        )
        for head in range(HEADS):
            stats_ref[head, :, rows_of(m)] = stats


def attend(info, vu, other, weights):
    half = CHIPS * ROWS
    return pl.pallas_call(
        attend_kernel,
        out_shape=[
            jax.ShapeDtypeStruct((HEAD_DIM, half), F32),
            jax.ShapeDtypeStruct((HEADS, 4, half), F32),
        ],
        in_specs=[sspec(), vspec(), vspec(), hspec()],
        out_specs=[vspec(), vspec()],
        scratch_shapes=[
            VMEM((2 * half, HEAD_DIM), BF16),
            VMEM((HEAD_DIM, 2 * half), BF16),
            VMEM((TILES, KEY_TILE, ROWS), BF16),
            pltpu.SemaphoreType.DMA((CHIPS,)),
        ],
        compiler_params=params(ATTN),
        cost_estimate=attention_cost(1, 0),
        name="attend",
    )(info, vu, other, weights)


def back_v_kernel(
    info,
    vu_ref,
    att_ref,
    stats_ref,
    weight_hbm,
    out_ref,
    sib_ref,
    grad_t_ref,
    grad_ref,
    dv_ref,
    weight_ref,
    sems,
):
    length, core = info[0], info[1]
    arrive = fetch_tiles(length, weight_hbm, weight_ref, sems)
    width = HEADS * HEAD_DIM
    stat = [[stats_ref[head, s : s + 1, :] for s in range(4)] for head in range(HEADS)]
    mean = sum(row[0] for row in stat) * (1.0 / HEADS)
    square = sum(row[1] + HEAD_DIM * (row[0] - mean) * (row[0] - mean) for row in stat)
    inverse = lax.rsqrt(square * (1.0 / width) + EPSILON)
    up_mean = sum(row[2] for row in stat) * (1.0 / width)
    cross = sum(row[3] + (row[0] - mean) * row[2] for row in stat) * inverse * (1.0 / width)
    for m in range(CHIPS):
        where = rows_of(m)
        up = vu_ref[m, 1].T.astype(F32)
        hat = (att_ref[:, where] - mean[:, where]) * inverse[:, where]
        out_ref[m, 1] = hat.astype(BF16).T
        grad = inverse[:, where] * (up - up_mean[:, where] - hat * cross[:, where])
        grad = grad.astype(BF16)
        grad_t_ref[:, where] = grad
        grad_ref[where, :] = grad.T

    def work(j):
        arrive(j)
        for m in range(j, CHIPS):
            term = dot(weight_ref[tile_of(j, m)], grad_ref[rows_of(m), :])
            if m == j:
                dv_ref[keys_of(j), :] = term
            else:
                dv_ref[keys_of(j), :] += term

    def dead(j):
        dv_ref[keys_of(j), :] = jnp.zeros((KEY_TILE, HEAD_DIM), F32)

    each_tile(length, work, dead)
    share(core, dv_ref, 1.0, out_ref, sib_ref)


def share(core, sum_ref, scale, out_ref, sib_ref):
    for chip in range(CHIPS):
        kept = pl.ds(pl.multiple_of((2 * chip + core) * ROWS, ROWS), ROWS)
        sent = pl.ds(pl.multiple_of((2 * chip + 1 - core) * ROWS, ROWS), ROWS)
        out_ref[chip, 0] = (sum_ref[kept, :] * scale).astype(BF16)
        sib_ref[chip] = (sum_ref[sent, :] * scale).astype(BF16)


def back_v(info, vu, att, stats, weights):
    half = CHIPS * ROWS
    return pl.pallas_call(
        back_v_kernel,
        out_shape=[
            jax.ShapeDtypeStruct((CHIPS, 2, ROWS, HEAD_DIM), BF16),
            jax.ShapeDtypeStruct((CHIPS, ROWS, HEAD_DIM), BF16),
            jax.ShapeDtypeStruct((HEAD_DIM, half), BF16),
        ],
        in_specs=[sspec(), vspec(), vspec(), vspec(), hspec()],
        out_specs=[vspec(), vspec(), vspec()],
        scratch_shapes=[
            VMEM((half, HEAD_DIM), BF16),
            VMEM((2 * half, HEAD_DIM), F32),
            VMEM((TILES, KEY_TILE, ROWS), BF16),
            pltpu.SemaphoreType.DMA((CHIPS,)),
        ],
        compiler_params=params(ATTN),
        cost_estimate=attention_cost(1, 0),
        name="back_v",
    )(info, vu, att, stats, weights)


def back_kq_kernel(
    info,
    kq_ref,
    vu_ref,
    other_ref,
    other_key_ref,
    slope_hbm,
    grad_t_ref,
    out_ref,
    sib_ref,
    value_ref,
    key_t_ref,
    dq_ref,
    dk_ref,
    slope_ref,
    sems,
):
    length, core = info[0], info[1]
    arrive = fetch_tiles(length, slope_hbm, slope_ref, sems)
    lay_rows(info, vu_ref, other_ref, value_ref)
    dq_ref[...] = jnp.zeros_like(dq_ref)
    for chip in range(CHIPS):
        for rows, side in ((kq_ref[chip, 0], core), (other_key_ref[chip], 1 - core)):
            start = pl.multiple_of((2 * chip + side) * ROWS, ROWS)
            key_t_ref[:, pl.ds(start, ROWS)] = rows.T

    def work(j):
        arrive(j)
        for m in range(j, CHIPS):
            grad = dot(value_ref[keys_of(j), :], grad_t_ref[:, rows_of(m)])
            slope = slope_ref[tile_of(j, m)].astype(F32)
            slope_ref[tile_of(j, m)] = (grad * slope).astype(BF16)
        for m in range(j, CHIPS):
            grad = slope_ref[tile_of(j, m)]
            dk = dot(grad, kq_ref[m, 1])
            dq = dot(key_t_ref[:, keys_of(j)], grad)
            if m == j:
                dk_ref[keys_of(j), :] = dk
            else:
                dk_ref[keys_of(j), :] += dk
            dq_ref[:, rows_of(m)] += dq

    def dead(j):
        dk_ref[keys_of(j), :] = jnp.zeros((KEY_TILE, HEAD_DIM), F32)

    each_tile(length, work, dead)
    for m in range(CHIPS):
        out_ref[m, 1] = (dq_ref[:, rows_of(m)] * SCALE).astype(BF16).T
    share(core, dk_ref, SCALE, out_ref, sib_ref)


def back_kq(info, kq, vu, other, other_keys, slope, grad_t):
    half = CHIPS * ROWS
    return pl.pallas_call(
        back_kq_kernel,
        out_shape=[
            jax.ShapeDtypeStruct((CHIPS, 2, ROWS, HEAD_DIM), BF16),
            jax.ShapeDtypeStruct((CHIPS, ROWS, HEAD_DIM), BF16),
        ],
        in_specs=[sspec()] + [vspec()] * 4 + [hspec(), vspec()],
        out_specs=[vspec(), vspec()],
        scratch_shapes=[
            VMEM((2 * half, HEAD_DIM), BF16),
            VMEM((HEAD_DIM, 2 * half), BF16),
            VMEM((HEAD_DIM, half), F32),
            VMEM((2 * half, HEAD_DIM), F32),
            VMEM((TILES, KEY_TILE, ROWS), BF16),
            pltpu.SemaphoreType.DMA((CHIPS,)),
        ],
        compiler_params=params(ATTN),
        cost_estimate=attention_cost(3, 0),
        name="back_kq",
    )(info, kq, vu, other, other_keys, slope, grad_t)


def merge_kernel(out_ref, sib_ref, *refs):
    done_ref = refs[-1]
    done_ref[:, 0] = (out_ref[:, 0].astype(F32) + sib_ref[...].astype(F32)).astype(BF16)
    done_ref[:, 1] = out_ref[:, 1]


def merge(out, sib, *kept):
    return pl.pallas_call(
        merge_kernel,
        out_shape=jax.ShapeDtypeStruct(out.shape, out.dtype),
        in_specs=[vspec(), vspec()] + [vspec() for _ in kept],
        out_specs=vspec(),
        compiler_params=params(SMALL),
        name="merge",
    )(out, sib, *kept)


def gather(back_ref, part, chunk):
    heads = CHUNK // HEAD_DIM
    blocks = [back_ref[chunk * heads + head, part].astype(F32) for head in range(heads)]
    return jnp.concatenate(blocks, axis=1)


def finish_vg_kernel(
    back_ref,
    gate_ref,
    slope_ref,
    hist_ref,
    up_ref,
    w_hbm,
    w_out_ref,
    mixed_ref,
    sum_ref,
    w_ref,
    sems,
):
    width = hist_ref.shape[1]
    arrive = start_weights(w_hbm, w_ref, sems, (1, 0))
    mixed = hist_ref[...].astype(F32)
    total = jnp.zeros(hist_ref.shape, F32)
    for part in range(2):
        for chunk, columns in chunks(width):
            grad = gather(back_ref, part, chunk)
            if part:
                gated = (grad * gate_ref[:, columns].astype(F32)).astype(BF16)
                mixed = mixed + dot(gated, w_out_ref[columns, :])
                grad = grad * up_ref[:, columns]
            pre = (grad * slope_ref[part, :, columns].astype(F32)).astype(BF16)
            arrive(part, chunk)
            total = total + dot_nt(pre, w_ref[part * (width // CHUNK) + chunk])
    mixed_ref[...] = mixed.astype(BF16)
    sum_ref[...] = total


def finish_vg(back, gate, slope, history, upstream, w_in, w_out):
    rows, width = history.shape
    return pl.pallas_call(
        finish_vg_kernel,
        in_specs=[vspec()] * 5 + [hspec(), vspec()],
        out_specs=[vspec(), vspec()],
        scratch_shapes=weight_scratch(width),
        out_shape=[
            jax.ShapeDtypeStruct((rows, width), BF16),
            jax.ShapeDtypeStruct((rows, width), F32),
        ],
        compiler_params=params(DENSE),
        name="finish_vg",
    )(back, gate, slope, history, upstream, w_in, w_out)


def finish_kq_kernel(
    back_in,
    slope_in,
    hist_in,
    start_in,
    cot_in,
    place_ref,
    w_hbm,
    rows_ref,
    w_ref,
    sems,
    back_ref,
    slope_ref,
    hist_ref,
    start_ref,
    cot_ref,
    in_sems,
):
    width = hist_ref.shape[1]
    pairs = [
        (hist_in, hist_ref),
        (back_in, back_ref),
        (slope_in, slope_ref),
        (start_in, start_ref),
        (cot_in, cot_ref),
    ]
    copies = [pltpu.make_async_copy(a, b, in_sems.at[i]) for i, (a, b) in enumerate(pairs)]
    for copy in copies[:3]:
        copy.start()
    arrive = start_weights(w_hbm, w_ref, sems, (3, 2))
    for copy in copies[3:]:
        copy.start()
    copies[0].wait()
    hat, inverse = normalize(hist_ref[...].astype(F32))
    copies[1].wait()
    copies[2].wait()
    grad = jnp.zeros(hist_ref.shape, F32)
    for part in range(2):
        for chunk, columns in chunks(width):
            pre = gather(back_ref, part, chunk) * slope_ref[part, :, columns].astype(F32)
            arrive(part, chunk)
            grad = grad + dot_nt(pre.astype(BF16), w_ref[part * (width // CHUNK) + chunk])
    copies[3].wait()
    grad = grad + start_ref[...]
    grad = inverse * (grad - row_mean(grad) - hat * row_mean(grad * hat))
    copies[4].wait()
    grad = (grad + cot_ref[...].astype(F32)).astype(BF16)
    rows_ref[...] = dot(onehot(place_ref[...]), grad).astype(BF16).reshape(rows_ref.shape)


def finish_kq(back, slope, history, start, cotangent, place, w_in):
    rows, width = history.shape
    return pl.pallas_call(
        finish_kq_kernel,
        in_specs=[hspec()] * 5 + [vspec(), hspec()],
        out_specs=vspec(),
        scratch_shapes=weight_scratch(width)
        + [
            VMEM((CHIPS, 2, ROWS, HEAD_DIM), BF16),
            VMEM((2, rows, width), BF16),
            VMEM((rows, width), BF16),
            VMEM((rows, width), F32),
            VMEM((rows, width), BF16),
            pltpu.SemaphoreType.DMA((5,)),
        ],
        out_shape=jax.ShapeDtypeStruct((rows // 2, 2, width), BF16),
        compiler_params=params(52),
        name="finish_kq",
    )(back, slope, history, start, cotangent, place, w_in)


def body(log_rows, send_order, place, hist_len, w_in, w_out, cotangent):
    seq_size = lax.axis_size("seq")
    seq_index = lax.axis_index("seq")
    spot = seq_index % GROUP
    length = jnp.take(hist_len[0], seq_index // GROUP)
    info = jnp.stack([length, spot % 2]).astype(jnp.int32)
    same_core = [list(range(g + c, g + GROUP, 2)) for g in range(0, seq_size, GROUP) for c in (0, 1)]
    swap = [(i, i ^ 1) for i in range(seq_size)]

    def to_all(block):
        return lax.all_to_all(block, ("dp", "seq"), split_axis=0, concat_axis=0, tiled=True)

    def to_group(block, members):
        return lax.all_to_all(
            block, "seq", split_axis=0, concat_axis=0, tiled=True, axis_index_groups=members
        )

    upstream = jnp.dot(cotangent, w_out.T, preferred_element_type=F32)
    arrived = to_all(pick_rows(log_rows, send_order))
    history, normed, slope_kq, kq = project_kq(info, arrived, place, w_in, upstream)
    kq = to_group(kq, same_core)
    gate, slope_vg, vu, token = project_vu(normed, w_in, upstream)
    other_keys = lax.ppermute(first_part(kq, token), "seq", swap)
    weights, slopes, token = weigh(info, kq, other_keys, token)
    vu = to_group(vu, same_core)
    other_values = lax.ppermute(first_part(vu, token), "seq", swap)
    att, stats = attend(info, vu, other_values, weights)
    stats = to_group(stats, same_core)
    out, sib, grad_t = back_v(info, vu, att, stats, weights)
    back_vh = merge(out, lax.ppermute(sib, "seq", swap), grad_t)
    out, sib = back_kq(info, kq, vu, other_values, other_keys, slopes, grad_t)
    back_vh = to_group(back_vh, same_core)
    back_kq_rows = merge(out, lax.ppermute(sib, "seq", swap))
    mixed, start = finish_vg(back_vh, gate, slope_vg, history, upstream, w_in, w_out)
    back_kq_rows = to_group(back_kq_rows, same_core)
    grads = finish_kq(back_kq_rows, slope_kq, history, start, cotangent, place, w_in)
    log_grad = unpick_rows(to_all(grads), send_order, F32)
    return (mixed, log_grad)


def solution(mesh):
    rows = P(("dp", "seq"), None)
    return jax.shard_map(
        body,
        mesh=mesh,
        in_specs=(rows, rows, rows, P("dp", None), P(), P(), rows),
        out_specs=(rows, rows),
        check_vma=False,
    )
```
